512 devices in a mesh: seq: 16 (over z), mp: 8 (over x, core), dp: 4 (over y).
Axes of the slice: x: 4, y: 4, z: 16, core: 2. Of those that a mesh axis runs over, the one named last changes fastest.
Arguments:
- tokens: bfloat16 [4, 4096, 768], P('dp', 'seq'), may hold values from -6 to 6
- gain: float32 [768], replicated, may hold values from 0.5 to 1.5
- qkv_weight: bfloat16 [768, 3, 768], P(None, None, 'mp'), may hold values from -12 to 12
- out_weight: bfloat16 [768, 768], P('mp'), may hold values from -0.21875 to 0.21875
- counts: int32 [4], P('dp'), may hold values from 1 to 4096, 10240 in all
- grad_out: bfloat16 [4, 4096, 768], P('dp', 'seq'), may hold values from -6 to 6
Outputs:
- d_tokens: bfloat16 [4, 4096, 768], P('dp', 'seq', 'mp')
- d_qkv_weight: float32 [768, 3, 768], P(('seq', 'dp'), None, 'mp')
- d_out_weight: float32 [768, 768], P('mp', ('seq', 'dp'))
- d_gain: float32 [768], P('mp')
The draws below stay inside these ranges and needn't reach their ends.
All inputs are finite; a program needn't handle non-finite values. No bound on the sum of `counts` on one device may be relied on, other than what follows from the above.
Results may differ from the reference program's by a relative error of at most 0.02.
The reference program's roundings to bfloat16 on the way count: a program that leaves them out, or rounds other values in their place, can miss the bound.
Values may be sent and summed in bfloat16 or wider, within the bound.
A program may use at most 64 MiB of HBM per device.

```python
import math
import jax
import jax.numpy as jnp
import numpy as np
from jax import lax

EMBED_WIDTH = 768
HEADS = 16
HDIM = 48
DILATION_RATE = 2
TOK_DEV = 256
TILE_SLOTS = 4096
SLIDE_TOTAL = 4
N_SEQ = 16
N_MP = 8


def draw_tokens(key, part):
    key = jax.random.fold_in(key, 11)
    seed_key = jax.random.fold_in(key, 0)
    values = jax.random.normal(seed_key, (SLIDE_TOTAL, TILE_SLOTS, EMBED_WIDTH), jnp.float32)
    return jnp.clip(values, -6.0, 6.0).astype(jnp.bfloat16)


def draw_qkv_weight(key, part):
    key = jax.random.fold_in(key, 23)
    seed_key = jax.random.fold_in(key, 0)
    scaling = EMBED_WIDTH ** (-0.5)
    values = jax.random.normal(seed_key, (EMBED_WIDTH, 3, EMBED_WIDTH), jnp.float32) * scaling
    return jnp.clip(values, -12.0, 12.0).astype(jnp.bfloat16)


def raised(result, key, source, target, shards_of, factor):
    owner, partner = [(jnp.arange(result.shape[axis_at]) // (result.shape[axis_at] // shards_of)).reshape([-1 if axis == axis_at else 1 for axis in range(result.ndim)]) for axis_at in (source, target)]
    chosen = jax.random.permutation(key, shards_of)[partner]
    strong = (owner == chosen) | (owner == (partner + shards_of // 2) % shards_of)
    return jnp.where(strong, factor * result, result)


def block_levels(stream_key, shape, cuts, smallest, largest):
    factor_of = 1.0
    for axis_at, shards_of in cuts:
        steps = jax.random.uniform(jax.random.fold_in(jax.random.fold_in(stream_key, 6), axis_at), (shards_of,), jnp.float32, smallest / len(cuts), largest / len(cuts))
        factor_of = factor_of * jnp.repeat(jnp.exp(steps), shape[axis_at] // shards_of).reshape((-1,) + (1,) * (len(shape) - 1 - axis_at))
    return factor_of


def length_profile(amount, total, limit, lean):
    portions = [(1 << 20) // math.isqrt(standing ** lean) + 1 for standing in range(2, amount + 1)]
    spare, given = total - limit - (amount - 1), [1] * (amount - 1)
    while spare > 0:
        free = [i for i in range(amount - 1) if given[i] < limit]
        whole, budget = sum([portions[i] for i in free]), spare
        for i in free:
            extra = min(limit - given[i], max(1, budget * portions[i] // whole), spare)
            given[i] = given[i] + extra
            spare = spare - extra
    return np.array([limit] + given)


def uneven(own_key, count, total, limit, lean):
    if count == 2:
        one = jax.random.randint(own_key, (), max(1, total - limit), min(limit, total - 1) + 1)
        return jnp.stack([one, total - one])
    sizes = jnp.asarray(length_profile(count, total, limit, lean), jnp.int32)
    pairs = (count - 1) // 2
    donor, taker = sizes[1:1 + 2 * pairs:2], sizes[2:2 + 2 * pairs:2]
    room = jnp.minimum(donor - 1, limit - taker)
    passed = jax.random.randint(jax.random.fold_in(own_key, 1), (pairs,), 0, 1 << 20) % (room + 1)
    sizes = sizes.at[1:1 + 2 * pairs:2].set(donor - passed).at[2:2 + 2 * pairs:2].set(taker + passed)
    return sizes[jax.random.permutation(jax.random.fold_in(own_key, 2), count)]


def normal_values(own_key, shape, spread, reach, cuts=(), held_as=jnp.bfloat16):
    entries = jax.random.normal(own_key, shape, jnp.float32) * spread
    if len(cuts) > 0:
        entries = block_levels(own_key, shape, cuts, -0.22, 0.18) * entries
    return jnp.clip(entries, min=-reach, max=reach).astype(held_as)


def heavy_noise(key, extent, spread, limit, pieces, heavy, held_as=jnp.bfloat16):
    entries = spread * jax.random.normal(key, extent, jnp.float32)
    if pieces:
        entries = entries * block_levels(key, extent, pieces, -0.22, 0.18)
    return jnp.clip(raised(entries, jax.random.fold_in(key, 3), *heavy), -limit, limit).astype(held_as)


def setup_inputs(seed: int = 0) -> dict:
    arg_keys = jax.random.split(jax.random.key(seed), 7)
    return {
        "tokens": draw_tokens(jax.random.fold_in(arg_keys[6], 71), 0),
        "gain": jnp.clip(jax.random.uniform(arg_keys[1], (EMBED_WIDTH,), jnp.float32, 0.5, 1.5), 0.5, 1.5),
        "qkv_weight": draw_qkv_weight(jax.random.fold_in(arg_keys[6], 71), 0),
        "out_weight": normal_values(arg_keys[3], (EMBED_WIDTH, EMBED_WIDTH), EMBED_WIDTH ** -0.5, 0.21875, ((0, 8),)),
        "counts": uneven(arg_keys[4], SLIDE_TOTAL, TILE_SLOTS * (SLIDE_TOTAL + 1) // 2, TILE_SLOTS, 2).astype(jnp.int32),
        "grad_out": heavy_noise(arg_keys[5], (SLIDE_TOTAL, TILE_SLOTS, EMBED_WIDTH), 1.0, 6.0, ((0, 4), (1, 16)), (1, 2, 16, 2.0)),
    }


far_below = -1e+30

def contract(form, left_op, right_op):
    return jnp.einsum(form, left_op.astype(jnp.float32), right_op.astype(jnp.float32))

def pick_rows(value_array):
    count_heads, slide_length = (value_array.shape[0], value_array.shape[1])
    trailing_part = value_array.shape[2:]
    folded_key = value_array.reshape((count_heads // DILATION_RATE, DILATION_RATE, slide_length // DILATION_RATE, DILATION_RATE) + trailing_part)
    picked_rows = jnp.diagonal(folded_key, axis1=1, axis2=3)
    picked_rows = jnp.moveaxis(picked_rows, -1, 1)
    return picked_rows.reshape((count_heads, slide_length // DILATION_RATE) + trailing_part)

def insert_rows(value_array, slide_length):
    count_heads = value_array.shape[0]
    trailing_part = value_array.shape[2:]
    folded_key = value_array.reshape((count_heads // DILATION_RATE, DILATION_RATE, slide_length // DILATION_RATE, 1) + trailing_part)
    index_rows = lax.broadcasted_iota(jnp.int32, (DILATION_RATE, DILATION_RATE), 0)
    column_index = lax.broadcasted_iota(jnp.int32, (DILATION_RATE, DILATION_RATE), 1)
    identity_matrix = (index_rows == column_index).astype(value_array.dtype)
    identity_matrix = identity_matrix.reshape((1, DILATION_RATE, 1, DILATION_RATE) + (1,) * len(trailing_part))
    return (folded_key * identity_matrix).reshape((count_heads, slide_length) + trailing_part)

def attend_block(queries, keys_near, values_near, keys_far, values_far, grad_attend, live_rows, live_far):
    count_heads, slide_length, depth = queries.shape
    scaling = 1.0 / math.sqrt(depth)
    near_score = jnp.where(live_rows[None, None, :], contract('hqe,hke->hqk', queries, keys_near) * scaling, far_below)
    far_queries = pick_rows(queries)
    far_score = jnp.where(live_far[:, None, :], contract('hqe,hke->hqk', far_queries, keys_far) * scaling, far_below)
    near_top = lax.optimization_barrier(jnp.max(near_score, axis=2))
    far_top = jnp.maximum(pick_rows(near_top), lax.optimization_barrier(jnp.max(far_score, axis=2)))
    selected_rows = insert_rows(jnp.ones((count_heads, slide_length // DILATION_RATE), jnp.float32), slide_length) > 0.5
    row_top = jnp.where(selected_rows, insert_rows(far_top, slide_length), near_top)
    near_exp = jnp.exp(near_score - row_top[:, :, None])
    far_exp = jnp.exp(far_score - far_top[:, :, None])
    totals = lax.optimization_barrier(jnp.sum(near_exp, axis=2)) + insert_rows(lax.optimization_barrier(jnp.sum(far_exp, axis=2)), slide_length)
    live_grid = jnp.broadcast_to(live_rows[None, :], (count_heads, slide_length))
    near_weight = jnp.where(live_grid[:, :, None], near_exp / totals[:, :, None], 0.0)
    far_weight = jnp.where(pick_rows(live_grid)[:, :, None], far_exp / pick_rows(totals)[:, :, None], 0.0)
    near_bar = near_weight.astype(jnp.bfloat16)
    far_bar = far_weight.astype(jnp.bfloat16)
    attended = contract('hqk,hke->hqe', near_bar, values_near)
    attended = attended + insert_rows(contract('hqk,hke->hqe', far_bar, values_far), slide_length)
    attended = attended.astype(jnp.bfloat16)
    far_grad = pick_rows(grad_attend)
    near_prob = contract('hqe,hke->hqk', grad_attend, values_near)
    far_prob = contract('hqe,hke->hqk', far_grad, values_far)
    deltas = lax.optimization_barrier(jnp.sum(near_weight * near_prob, axis=2)) + insert_rows(lax.optimization_barrier(jnp.sum(far_weight * far_prob, axis=2)), slide_length)
    near_ds = (near_weight * (near_prob - deltas[:, :, None]) * scaling).astype(jnp.bfloat16)
    far_ds = (far_weight * (far_prob - pick_rows(deltas)[:, :, None]) * scaling).astype(jnp.bfloat16)
    d_query = contract('hqk,hke->hqe', near_ds, keys_near)
    d_query = d_query + insert_rows(contract('hqk,hke->hqe', far_ds, keys_far), slide_length)
    d_key = contract('hqk,hqe->hke', near_ds, queries)
    d_value = contract('hqk,hqe->hke', near_bar, grad_attend)
    far_dkey = contract('hqk,hqe->hke', far_ds, far_queries)
    far_dvalue = contract('hqk,hqe->hke', far_bar, far_grad)
    return (attended, d_query, d_key, d_value, far_dkey, far_dvalue)

def reference(tokens, gain, qkv_weight, out_weight, counts, grad_out):
    sparse_length = TILE_SLOTS // DILATION_RATE
    positions = jnp.arange(TILE_SLOTS, dtype=jnp.int32)
    sparse_positions = pick_rows(jnp.broadcast_to(positions[None, :], (HEADS, TILE_SLOTS)))
    flat_weight = qkv_weight.reshape(EMBED_WIDTH, 3 * EMBED_WIDTH)
    grouped_weight = qkv_weight.reshape(EMBED_WIDTH, 3, N_MP, EMBED_WIDTH // N_MP)

    def one_slide(carry, inputs):
        slide_tokens, slide_grad, slide_count = inputs
        widened = slide_tokens.astype(jnp.float32)
        centered = widened - lax.optimization_barrier(jnp.mean(widened, axis=1, keepdims=True))
        inverse_std = lax.rsqrt(lax.optimization_barrier(jnp.mean(centered * centered, axis=1, keepdims=True)) + 1e-05)
        normal_form = centered * inverse_std
        normed = (normal_form * gain[None, :]).astype(jnp.bfloat16)
        projected = jnp.dot(normed, flat_weight, preferred_element_type=jnp.float32).astype(jnp.bfloat16)
        split_heads = projected.reshape(TILE_SLOTS, 3, HEADS, HDIM).transpose(1, 2, 0, 3)
        queries, keys_all, values_all = (split_heads[0], split_heads[1], split_heads[2])
        grad_attend = jnp.dot(slide_grad, out_weight.T, preferred_element_type=jnp.float32).astype(jnp.bfloat16)
        grad_attend = grad_attend.reshape(TILE_SLOTS, HEADS, HDIM).transpose(1, 0, 2)
        live_all = positions < slide_count
        live_far = sparse_positions < slide_count
        keys_far = pick_rows(keys_all)
        values_far = pick_rows(values_all)

        def one_block(far_total, block_index):
            block_start = block_index * TOK_DEV

            def take_block(value_array):
                return lax.dynamic_slice_in_dim(value_array, block_start, TOK_DEV, 1)
            live_rows = lax.dynamic_slice_in_dim(live_all, block_start, TOK_DEV, 0)
            results = attend_block(take_block(queries), take_block(keys_all), take_block(values_all), keys_far, values_far, take_block(grad_attend), live_rows, live_far)
            far_terms = jnp.stack([results[4], results[5]]).astype(jnp.bfloat16)
            far_terms = lax.optimization_barrier(far_terms).astype(jnp.float32)
            return (far_total + far_terms, results[:4])
        start_total = jnp.zeros((2, HEADS, sparse_length, HDIM), jnp.float32)
        far_total, block_out = lax.scan(one_block, start_total, jnp.arange(N_SEQ, dtype=jnp.int32))

        def merge_blocks(stacked):
            return stacked.transpose(1, 0, 2, 3).reshape(HEADS, TILE_SLOTS, HDIM)
        attended = merge_blocks(block_out[0]).transpose(1, 0, 2).reshape(TILE_SLOTS, EMBED_WIDTH)
        d_query = merge_blocks(block_out[1])
        d_key = merge_blocks(block_out[2]) + insert_rows(far_total[0], TILE_SLOTS)
        d_value = merge_blocks(block_out[3]) + insert_rows(far_total[1], TILE_SLOTS)
        d_proj = jnp.stack([d_query, d_key, d_value]).astype(jnp.bfloat16)
        d_proj = d_proj.transpose(2, 0, 1, 3).reshape(TILE_SLOTS, 3, EMBED_WIDTH)
        out_term = jnp.dot(attended.T, slide_grad, preferred_element_type=jnp.float32)
        qkv_term = jnp.einsum('td,tcf->dcf', normed.astype(jnp.float32), d_proj.astype(jnp.float32))
        grouped_grad = d_proj.reshape(TILE_SLOTS, 3, N_MP, EMBED_WIDTH // N_MP)

        def one_group(total_grad, group_index):
            grad_piece = lax.dynamic_index_in_dim(grouped_grad, group_index, 2, keepdims=False)
            weight_piece = lax.dynamic_index_in_dim(grouped_weight, group_index, 2, keepdims=False)
            partial_grad = jnp.einsum('tcf,dcf->td', grad_piece.astype(jnp.float32), weight_piece.astype(jnp.float32))
            partial_grad = lax.optimization_barrier(partial_grad.astype(jnp.bfloat16)).astype(jnp.float32)
            return (total_grad + partial_grad, None)
        d_normed = lax.scan(one_group, jnp.zeros((TILE_SLOTS, EMBED_WIDTH), jnp.float32), jnp.arange(N_MP, dtype=jnp.int32))[0]
        gain_term = lax.optimization_barrier(jnp.sum(d_normed * normal_form, axis=0))
        scaled = d_normed * gain[None, :]
        mean_scaled = lax.optimization_barrier(jnp.mean(scaled, axis=1, keepdims=True))
        mean_mixed = lax.optimization_barrier(jnp.mean(scaled * normal_form, axis=1, keepdims=True))
        d_tokens = slide_grad.astype(jnp.float32) + (scaled - mean_scaled - normal_form * mean_mixed) * inverse_std
        new_carry = (carry[0] + qkv_term, carry[1] + out_term, carry[2] + gain_term)
        return (new_carry, d_tokens.astype(jnp.bfloat16))
    start_carry = (jnp.zeros((EMBED_WIDTH, 3, EMBED_WIDTH), jnp.float32), jnp.zeros((EMBED_WIDTH, EMBED_WIDTH), jnp.float32), jnp.zeros((EMBED_WIDTH,), jnp.float32))
    totals, d_tokens = lax.scan(one_slide, start_carry, (tokens, grad_out, counts))
    return (d_tokens, totals[0], totals[1], totals[2])
```

```python
import functools
import math

import jax
import jax.numpy as jnp
from jax import lax
from jax.experimental import pallas as pl
from jax.experimental.pallas import tpu as pltpu
from jax.sharding import PartitionSpec as P

HDIM = 48
BLOCK = 256
HALF = BLOCK // 2
GROUP = 2 * HDIM
LANES = 128
MESH = pl.DeviceIdType.MESH
BF = jnp.bfloat16
F32 = jnp.float32
far_below = -1e30


def dot_nn(left, right):
    return lax.dot_general(left, right, (((1,), (0,)), ((), ())), preferred_element_type=F32)


def dot_nt(left, right):
    return lax.dot_general(left, right, (((1,), (1,)), ((), ())), preferred_element_type=F32)


def iota(shape, axis):
    return lax.broadcasted_iota(jnp.int32, shape, axis)


def one_hot(condition):
    return jnp.where(condition, 1.0, 0.0).astype(BF)


def row_sum(value):
    return jnp.sum(value, axis=1, keepdims=True)


def floor_div(value, by):
    return jnp.floor((value + 0.5) * (1.0 / by))


def layer_kernel(
    n_seq, n_mp, n_dp,
    counts, tokens, grad_out, gain, weight, out_weight,
    tok_out, early_out, late_out, gain_out,
    kv_far, scores, probs, top, kv_here, q_here, da_here, q_rows, da_rows,
    near_scores, near_probs, normed_s, go_s, normed_p, go_p, gain_pad, mixed_pad, weight_pad,
    contrib, far_send, far_recv, d_parts, own_parts,
    y_send, y_recv, z_send, z_recv, mp_send, mp_recv, gy_send, gy_recv, gz_send, gz_recv,
    ag_ss, ag_rs, rs_ss, rs_rs, y_ss, y_rs, z_ss, z_rs, mp_ss, mp_rs, gy_ss, gy_rs, gz_ss, gz_rs,
):
    width = n_mp * GROUP
    chunk = width // n_dp
    rows = chunk // n_seq
    rows_pad = -(-rows // 16) * 16
    mid = n_seq // 2
    scaling = 1.0 / math.sqrt(HDIM)
    s_me = lax.axis_index("seq")
    m_me = lax.axis_index("mp")
    d_me = lax.axis_index("dp")
    count = counts[0]

    def peer(axis, me, size, step):
        return {axis: lax.rem(me + (step + size), size)}

    barrier = pltpu.get_barrier_semaphore()
    for axis, me, size in (("seq", s_me, n_seq), ("dp", d_me, n_dp), ("mp", m_me, n_mp)):
        for step in range(1, size):
            pl.semaphore_signal(
                barrier, inc=1, device_id=peer(axis, me, size, step), device_id_type=MESH
            )

    def remote(src, dst, send, recv, device):
        return pltpu.make_async_remote_copy(
            src_ref=src, dst_ref=dst, send_sem=send, recv_sem=recv,
            device_id=device, device_id_type=MESH,
        )

    def position(shape, axis):
        at = iota(shape, axis)
        return 2 * (at % HALF) + at // HALF

    order = one_hot(position((BLOCK, BLOCK), 0) == iota((BLOCK, BLOCK), 1))
    eye = one_hot(iota((BLOCK, BLOCK), 0) == iota((BLOCK, BLOCK), 1))

    x = dot_nn(order, tokens[...])
    mean = row_sum(x) * (1.0 / width)
    centered = x - mean
    inverse_std = lax.rsqrt(row_sum(centered * centered) * (1.0 / width) + 1e-05)
    normal_form = centered * inverse_std
    scaled_form = normal_form * gain[...]
    normed = scaled_form.astype(BF)
    normed_s[...] = normed
    kv_here[...] = dot_nt(weight[GROUP:, :], normed).astype(BF)
    for part in range(2):
        for h in range(2):
            at = pl.ds(part * GROUP + h * HDIM, HDIM)
            kv_far[mid, at, :] = kv_here[at, h * HALF : (h + 1) * HALF]

    pl.semaphore_wait(barrier, n_seq + n_dp + n_mp - 3)

    right = peer("seq", s_me, n_seq, 1)
    left = peer("seq", s_me, n_seq, -1)

    def gather_copy(way, step, piece):
        source = mid - step if way == 0 else mid + step
        target = source - 1 if way == 0 else source + 1
        at = pl.ds(piece * GROUP, GROUP)
        return remote(
            kv_far.at[source, at], kv_far.at[target, at],
            ag_ss.at[way, step, piece], ag_rs.at[way, step, piece],
            right if way == 0 else left,
        )

    steps = (mid, mid - 1)
    for piece in range(2):
        for way in range(2):
            if steps[way] > 0:
                gather_copy(way, 0, piece).start()

    for m in range(n_mp):
        to, of = pl.ds(m * LANES, GROUP), slice(m * GROUP, (m + 1) * GROUP)
        rest = pl.ds(m * LANES + GROUP, LANES - GROUP)
        mixed_pad[:, to] = scaled_form[:, of]
        mixed_pad[:, rest] = jnp.zeros((BLOCK, LANES - GROUP), F32)
        gain_pad[:, to] = gain[:, of]
        gain_pad[:, rest] = jnp.zeros((1, LANES - GROUP), F32)
    q_here[...] = dot_nt(weight[:GROUP, :], normed).astype(BF)
    go_s[...] = dot_nn(order, grad_out[...]).astype(BF)
    da_here[...] = dot_nt(out_weight[...], go_s[...]).astype(BF)
    live_key = s_me * BLOCK + position((1, BLOCK), 1) < count
    live_query = s_me * BLOCK + position((BLOCK, 1), 0) < count

    def head(h, part=0):
        return slice(part * GROUP + h * HDIM, part * GROUP + (h + 1) * HDIM)

    def far_at(h):
        return slice(h * HALF, (h + 1) * HALF)

    for h in range(2):
        q_rows[h] = dot_nt(eye, q_here[head(h), :]).astype(BF)
        da_rows[h] = dot_nt(eye, da_here[head(h), :]).astype(BF)
        near_scores[h] = jnp.where(
            live_key, dot_nn(q_rows[h], kv_here[head(h), :]) * scaling, far_below
        )
        near_probs[h] = dot_nn(da_rows[h], kv_here[head(h, 1), :])
        top[h] = jnp.maximum(
            near_scores[h, far_at(h), :HALF], near_scores[h, far_at(h), HALF:]
        )

    def far_scores(slot):
        owner = lax.rem(s_me + (slot - mid + n_seq), n_seq)
        for h in range(2):
            live = owner * BLOCK + 2 * iota((1, HALF), 1) + h < count
            score = dot_nn(q_rows[h, far_at(h), :], kv_far[slot, head(h), :]) * scaling
            score = jnp.where(live, score, far_below)
            scores[h, slot] = score
            top[h] = jnp.maximum(top[h], score)
            probs[h, slot] = dot_nn(da_rows[h, far_at(h), :], kv_far[slot, head(h, 1), :])

    place = iota((width, 1), 0).astype(F32)
    piece_at = floor_div(place, rows)
    dp_at = floor_div(piece_at, n_seq)
    feature = n_dp * rows * (piece_at - n_seq * dp_at) + rows * dp_at + (place - rows * piece_at)
    spread = one_hot(feature == iota((width, width), 1).astype(F32))

    def fill_normed():
        normed_p[...] = dot_nt(spread, normed_s[...]).astype(BF)

    def fill_go():
        go_p[...] = dot_nt(spread, go_s[...]).astype(BF)

    def fill_weight():
        for m in range(n_mp):
            weight_pad[:, m * LANES : m * LANES + GROUP] = weight[:, m * GROUP : (m + 1) * GROUP]
            weight_pad[:, m * LANES + GROUP : (m + 1) * LANES] = jnp.zeros(
                (3 * GROUP, LANES - GROUP), BF
            )

    def fill_own():
        mine = one_hot(
            (iota((width, LANES), 0) == m_me * GROUP + iota((width, LANES), 1))
            & (iota((width, LANES), 1) < GROUP)
        )
        own_parts[0] = dot_nn(go_s[...], mine)
        own_parts[1] = (dot_nn(dot_nn(order, tokens[...]).astype(BF), mine) - mean) * inverse_std
        for part in range(4):
            d_parts[part, GROUP:, :] = jnp.zeros((LANES - GROUP, BLOCK), BF)

    fillers = [fill_normed, fill_go, fill_weight, fill_own]
    far_scores(mid)
    for step in range(mid):
        for piece in range(2):
            for way in range(2):
                if step < steps[way]:
                    gather_copy(way, step, piece).wait_recv()
                    if step + 1 < steps[way]:
                        gather_copy(way, step + 1, piece).start()
        if step < len(fillers):
            fillers[step]()
        far_scores(mid - 1 - step)
        if step < steps[1]:
            far_scores(mid + 1 + step)
    for filler in fillers[mid:]:
        filler()

    inverse_total, deltas = [], []
    for h in range(2):
        far_top = jnp.max(top[h], axis=1, keepdims=True)
        total = jnp.zeros((HALF, HALF), F32)
        delta = jnp.zeros((HALF, HALF), F32)
        for slot in range(n_seq):
            grown = jnp.exp(scores[h, slot] - far_top)
            scores[h, slot] = grown
            total = total + grown
            delta = delta + grown * probs[h, slot]
        halves_total, halves_delta = [], []
        for half in range(2):
            at = far_at(half)
            near = near_scores[h, at, :]
            peak = far_top if half == h else jnp.max(near, axis=1, keepdims=True)
            grown = jnp.exp(near - peak)
            near_scores[h, at, :] = grown
            sums = row_sum(grown)
            mixed = row_sum(grown * near_probs[h, at, :])
            if half == h:
                sums = sums + row_sum(total)
                mixed = mixed + row_sum(delta)
            inverse = jnp.where(live_query[at, :], 1.0 / sums, 0.0)
            halves_total.append(inverse)
            halves_delta.append(mixed * inverse)
        inverse_total.append(halves_total)
        deltas.append(halves_delta)

    attended = [jnp.zeros((HDIM, HALF), F32) for _ in range(2)]
    d_query = [jnp.zeros((HDIM, HALF), F32) for _ in range(2)]

    def far_terms(slot):
        for h in range(2):
            weights = scores[h, slot] * inverse_total[h][h]
            bar = weights.astype(BF)
            ds = (weights * (probs[h, slot] - deltas[h][h]) * scaling).astype(BF)
            contrib[slot, head(h), :] = dot_nn(q_here[head(h), far_at(h)], ds)
            contrib[slot, head(h, 1), :] = dot_nn(da_here[head(h), far_at(h)], bar)
            attended[h] = attended[h] + dot_nt(kv_far[slot, head(h, 1), :], bar)
            d_query[h] = d_query[h] + dot_nt(kv_far[slot, head(h), :], ds)

    near_terms = []

    def near_part():
        for h in range(2):
            inverse = jnp.concatenate(inverse_total[h], axis=0)
            weights = near_scores[h] * inverse
            bar = weights.astype(BF)
            delta = jnp.concatenate(deltas[h], axis=0)
            ds = (weights * (near_probs[h] - delta) * scaling).astype(BF)
            d_key = dot_nn(q_here[head(h), :], ds)
            d_value = dot_nn(da_here[head(h), :], bar)
            near_terms.append((d_key, d_value))
            near_att = dot_nt(kv_here[head(h, 1), :], bar)
            near_dq = dot_nt(kv_here[head(h), :], ds)
            for half in range(2):
                at = far_at(half)
                att, dq = near_att[:, at], near_dq[:, at]
                if half == h:
                    att, dq = att + attended[h], dq + d_query[h]
                d_parts[0, head(h), at] = att.astype(BF)
                d_parts[1, head(h), at] = dq.astype(BF)

    def y_copy(phase, step):
        to = lax.rem(d_me + step, n_dp)
        at = pl.ds(pl.multiple_of(to * chunk, 16), chunk)
        return remote(
            y_send.at[phase, at], y_recv.at[phase, step - 1],
            y_ss.at[phase, step - 1], y_rs.at[phase, step - 1], {"dp": to},
        )

    def z_copy(phase, step):
        to = lax.rem(s_me + step, n_seq)
        at = pl.ds(pl.multiple_of(to * rows_pad, 16), rows_pad)
        return remote(
            z_send.at[phase, at], z_recv.at[phase, step - 1],
            z_ss.at[phase, step - 1], z_rs.at[phase, step - 1], {"seq": to},
        )

    def y_start(phase, sides):
        for side, (left_side, part) in enumerate(sides):
            y_send[phase, :, side * LANES : (side + 1) * LANES] = dot_nt(
                left_side[...], d_parts[part]
            ).astype(BF)
        for step in range(1, n_dp):
            y_copy(phase, step).start()

    z_order = sorted(range(1, n_seq), key=lambda step: -min(step, n_seq - step))
    widen = one_hot(
        (iota((n_seq * rows_pad, chunk), 0) // rows_pad * rows
         + iota((n_seq * rows_pad, chunk), 0) % rows_pad == iota((n_seq * rows_pad, chunk), 1))
        & (iota((n_seq * rows_pad, chunk), 0) % rows_pad < rows)
    )

    def z_start(phase):
        mine = pl.ds(pl.multiple_of(d_me * chunk, 16), chunk)
        total = y_send[phase, mine, :].astype(F32)
        for step in range(1, n_dp):
            y_copy(phase, step).wait_recv()
            total = total + y_recv[phase, step - 1].astype(F32)
        z_send[phase] = dot_nn(widen, total.astype(BF)).astype(BF)
        for step in z_order:
            z_copy(phase, step).start()

    def z_end(phase, result):
        mine = pl.ds(pl.multiple_of(s_me * rows_pad, 16), rows_pad)
        total = z_send[phase, mine, :].astype(F32)
        for step in z_order[::-1]:
            z_copy(phase, step).wait_recv()
            total = total + z_recv[phase, step - 1].astype(F32)
        result[...] = total

    def far_copy(way, step, piece):
        at = pl.ds(piece * GROUP, GROUP)
        return remote(
            far_send.at[way, step, at], far_recv.at[way, step, at],
            rs_ss.at[way, step, piece], rs_rs.at[way, step, piece],
            right if way == 0 else left,
        )

    def owner_slot(way, step):
        return (step and n_seq - step) if way == 0 else 1 + step

    todo = [owner_slot(way, step) for step in range(mid) for way in range(2) if step < steps[way]]
    todo.append(mid)
    for step in range(mid):
        for _ in range(2 if step == 0 else 4):
            if todo:
                far_terms(todo.pop(0))
        for piece in range(2):
            at = pl.ds(piece * GROUP, GROUP)
            for way in range(2):
                if step < steps[way]:
                    part = contrib[owner_slot(way, step), at, :]
                    if step > 0:
                        far_copy(way, step - 1, piece).wait_recv()
                        part = part + far_recv[way, step - 1, at, :].astype(F32)
                    far_send[way, step, at, :] = part.astype(BF)
                    far_copy(way, step, piece).start()
        if not todo and not near_terms:
            near_part()
            y_start(0, ((go_p, 0), (normed_p, 1)))
    for piece in range(2):
        at = pl.ds(piece * GROUP, GROUP)
        for way in range(2):
            if steps[way] > 0:
                far_copy(way, steps[way] - 1, piece).wait_recv()
                contrib[mid, at, :] += far_recv[way, steps[way] - 1, at, :].astype(F32)
    for h in range(2):
        for part in range(2):
            for half in range(2):
                term = near_terms[h][part][:, far_at(half)]
                if half == h:
                    term = term + contrib[mid, head(h, part), :]
                d_parts[2 + part, head(h), far_at(half)] = term.astype(BF)

    y_start(1, ((normed_p, 2), (normed_p, 3)))
    d_rows = jnp.zeros((BLOCK, n_mp * LANES), F32)
    for part in range(3):
        d_part = dot_nt(eye, d_parts[1 + part, :GROUP, :]).astype(BF)
        d_rows = d_rows + dot_nn(d_part, weight_pad[part * GROUP : (part + 1) * GROUP, :])
    d_rows = d_rows.astype(BF).astype(F32)
    first = row_sum(d_rows * gain_pad[...])
    second = row_sum(d_rows * mixed_pad[...])
    lane = iota((BLOCK, LANES), 1)
    extra = jnp.zeros((BLOCK, LANES), F32)
    for at, value in ((GROUP, first), (GROUP + 2, second)):
        coarse = value.astype(BF).astype(F32)
        extra = jnp.where(lane == at, coarse, extra)
        extra = jnp.where(lane == at + 1, value - coarse, extra)
    for m in range(n_mp):
        mp_send[m] = (d_rows[:, m * LANES : (m + 1) * LANES] + extra).astype(BF)

    def mp_copy(step):
        to = lax.rem(m_me + step, n_mp)
        return remote(
            mp_send.at[to], mp_recv.at[step - 1], mp_ss.at[step - 1], mp_rs.at[step - 1], {"mp": to}
        )

    for step in range(1, n_mp):
        mp_copy(step).start()
    z_start(0)
    z_start(1)

    d_normed = mp_send[m_me].astype(F32)
    for step in range(1, n_mp):
        mp_copy(step).wait_recv()
        d_normed = d_normed + mp_recv[step - 1].astype(F32)
    form = own_parts[1]
    gy_send[...] = jnp.broadcast_to(jnp.sum(d_normed * form, axis=0, keepdims=True), (8, LANES))

    def gy_copy(step):
        return remote(
            gy_send, gy_recv.at[step - 1], gy_ss.at[step - 1], gy_rs.at[step - 1],
            peer("dp", d_me, n_dp, step),
        )

    def gz_copy(step):
        return remote(
            gz_send, gz_recv.at[step - 1], gz_ss.at[step - 1], gz_rs.at[step - 1],
            peer("seq", s_me, n_seq, step),
        )

    for step in range(1, n_dp):
        gy_copy(step).start()
    mean_scaled = (d_normed[:, GROUP : GROUP + 1] + d_normed[:, GROUP + 1 : GROUP + 2]) * (1.0 / width)
    mean_mixed = (d_normed[:, GROUP + 2 : GROUP + 3] + d_normed[:, GROUP + 3 : GROUP + 4]) * (1.0 / width)
    scaled = d_normed * gain_pad[:, pl.ds(pl.multiple_of(m_me * LANES, LANES), LANES)]
    d_tok = own_parts[0] + (scaled - mean_scaled - form * mean_mixed) * inverse_std
    back = one_hot(iota((BLOCK, BLOCK), 0) == position((BLOCK, BLOCK), 1))
    tok_out[...] = dot_nn(back, d_tok.astype(BF)).astype(BF)[:, :GROUP]
    total = gy_send[...]
    for step in range(1, n_dp):
        gy_copy(step).wait_recv()
        total = total + gy_recv[step - 1]
    gz_send[...] = total
    for step in z_order:
        gz_copy(step).start()
    z_end(0, early_out)
    z_end(1, late_out)
    for step in z_order[::-1]:
        gz_copy(step).wait_recv()
        total = total + gz_recv[step - 1]
    gain_out[...] = total

    for way in range(2):
        for step in range(steps[way]):
            for piece in range(2):
                gather_copy(way, step, piece).wait_send()
                far_copy(way, step, piece).wait_send()
    for step in range(1, n_dp):
        for phase in range(2):
            y_copy(phase, step).wait_send()
        gy_copy(step).wait_send()
    for step in range(1, n_mp):
        mp_copy(step).wait_send()
    for step in range(1, n_seq):
        for phase in range(2):
            z_copy(phase, step).wait_send()
        gz_copy(step).wait_send()


def per_device(n_seq, n_mp, n_dp, tokens, gain, qkv_weight, out_weight, counts, grad_out):
    width = n_mp * GROUP
    chunk = width // n_dp
    rows = chunk // n_seq
    rows_pad = -(-rows // 16) * 16
    mid = n_seq // 2
    weight = qkv_weight.transpose(1, 2, 0).reshape(3 * GROUP, width)
    vmem = pl.BlockSpec(memory_space=pltpu.VMEM)
    dma = pltpu.SemaphoreType.DMA
    scratch = [
        pltpu.VMEM((n_seq, 2 * GROUP, HALF), BF),
        pltpu.VMEM((2, n_seq, HALF, HALF), F32),
        pltpu.VMEM((2, n_seq, HALF, HALF), F32),
        pltpu.VMEM((2, HALF, HALF), F32),
        pltpu.VMEM((2 * GROUP, BLOCK), BF),
        pltpu.VMEM((GROUP, BLOCK), BF),
        pltpu.VMEM((GROUP, BLOCK), BF),
        pltpu.VMEM((2, BLOCK, HDIM), BF),
        pltpu.VMEM((2, BLOCK, HDIM), BF),
        pltpu.VMEM((2, BLOCK, BLOCK), F32),
        pltpu.VMEM((2, BLOCK, BLOCK), F32),
        pltpu.VMEM((BLOCK, width), BF),
        pltpu.VMEM((BLOCK, width), BF),
        pltpu.VMEM((width, BLOCK), BF),
        pltpu.VMEM((width, BLOCK), BF),
        pltpu.VMEM((1, n_mp * LANES), F32),
        pltpu.VMEM((BLOCK, n_mp * LANES), F32),
        pltpu.VMEM((3 * GROUP, n_mp * LANES), BF),
        pltpu.VMEM((n_seq, 2 * GROUP, HALF), F32),
        pltpu.VMEM((2, mid, 2 * GROUP, HALF), BF),
        pltpu.VMEM((2, mid, 2 * GROUP, HALF), BF),
        pltpu.VMEM((4, LANES, BLOCK), BF),
        pltpu.VMEM((2, BLOCK, LANES), F32),
        pltpu.VMEM((2, width, 2 * LANES), BF),
        pltpu.VMEM((2, n_dp - 1, chunk, 2 * LANES), BF),
        pltpu.VMEM((2, n_seq * rows_pad, 2 * LANES), BF),
        pltpu.VMEM((2, n_seq - 1, rows_pad, 2 * LANES), BF),
        pltpu.VMEM((n_mp, BLOCK, LANES), BF),
        pltpu.VMEM((n_mp - 1, BLOCK, LANES), BF),
        pltpu.VMEM((8, LANES), F32),
        pltpu.VMEM((n_dp - 1, 8, LANES), F32),
        pltpu.VMEM((8, LANES), F32),
        pltpu.VMEM((n_seq - 1, 8, LANES), F32),
    ]
    for shape in (
        (2, mid, 2), (2, mid, 2), (2, n_dp - 1), (2, n_seq - 1), (n_mp - 1,), (n_dp - 1,), (n_seq - 1,),
    ):
        scratch += [dma(shape), dma(shape)]
    d_tok, early, late, d_gain = pl.pallas_call(
        functools.partial(layer_kernel, n_seq, n_mp, n_dp),
        out_shape=(
            jax.ShapeDtypeStruct((BLOCK, GROUP), BF),
            jax.ShapeDtypeStruct((rows_pad, 2 * LANES), F32),
            jax.ShapeDtypeStruct((rows_pad, 2 * LANES), F32),
            jax.ShapeDtypeStruct((8, LANES), F32),
        ),
        in_specs=[pl.BlockSpec(memory_space=pltpu.SMEM)] + [vmem] * 5,
        out_specs=(vmem,) * 4,
        scratch_shapes=scratch,
        compiler_params=pltpu.CompilerParams(
            collective_id=0, has_side_effects=True, vmem_limit_bytes=48 * 1024 * 1024
        ),
    )(counts, tokens[0], grad_out[0], gain.reshape(1, width), weight, out_weight)
    d_qkv = jnp.stack(
        [early[:rows, LANES : LANES + GROUP], late[:rows, :GROUP], late[:rows, LANES : LANES + GROUP]],
        axis=1,
    )
    return (d_tok[None], d_qkv, early[:rows, :GROUP].T, d_gain[0, :GROUP])


def solution(mesh):
    sizes = (mesh.shape["seq"], mesh.shape["mp"], mesh.shape["dp"])
    placed = (
        P("dp", "seq", None),
        P(),
        P(None, None, "mp"),
        P("mp", None),
        P("dp"),
        P("dp", "seq", None),
    )
    return jax.shard_map(
        functools.partial(per_device, *sizes),
        mesh=mesh,
        in_specs=placed,
        out_specs=(
            P("dp", "seq", "mp"),
            P(("seq", "dp"), None, "mp"),
            P("mp", ("seq", "dp")),
            P("mp"),
        ),
        check_vma=False,
    )
```

```python
import functools
import math

import jax
import jax.numpy as jnp
from jax import lax
from jax.experimental import pallas as pl
from jax.experimental.pallas import tpu as pltpu
from jax.sharding import PartitionSpec as P

HDIM = 48
BLOCK = 256
HALF = BLOCK // 2
GROUP = 2 * HDIM
LANES = 128
VMEM_BYTES = 60 * 1024 * 1024
MESH = pl.DeviceIdType.MESH
BF = jnp.bfloat16
F32 = jnp.float32
far_below = -1e30


def dot_nn(left, right):
    return lax.dot_general(left, right, (((1,), (0,)), ((), ())), preferred_element_type=F32)


def dot_nt(left, right):
    return lax.dot_general(left, right, (((1,), (1,)), ((), ())), preferred_element_type=F32)


def iota(shape, axis):
    return lax.broadcasted_iota(jnp.int32, shape, axis)


def one_hot(condition):
    return jnp.where(condition, 1.0, 0.0).astype(BF)


def row_sum(value):
    return jnp.sum(value, axis=1, keepdims=True)


def floor_div(value, by):
    return jnp.floor((value + 0.5) * (1.0 / by))


def layer_kernel(
    n_seq, n_mp, n_dp,
    counts, tokens_hbm, grad_hbm, gain_hbm, weight_hbm, out_weight_hbm,
    tok_out, early_out, late_out, gain_out,
    tokens, grad_out, gain, weight, out_weight,
    kv_far, qd_far, scores, probs, scores_t, probs_t, top, kv_here, qd_here, q_rows, da_rows, k_rows, v_rows,
    near_scores, near_probs, normed_s, go_s, normed_p, go_p, gain_pad, form_pad, weight_pad,
    d_parts, own_parts, stat_send, stat_recv,
    y_send, y_recv, z_send, z_recv, mp_send, mp_recv,
    gm_send, gm_recv, gy_send, gy_recv, gz_send, gz_recv,
    in_sem, kv_ss, kv_rs, qd_ss, qd_rs, st_ss, st_rs, y_ss, y_rs, z_ss, z_rs, mp_ss, mp_rs,
    gm_ss, gm_rs, gy_ss, gy_rs, gz_ss, gz_rs,
):
    width = n_mp * GROUP
    chunk = width // n_dp
    rows = chunk // n_seq
    rows_pad = -(-rows // 16) * 16
    mid = n_seq // 2
    scaling = 1.0 / math.sqrt(HDIM)
    s_me = lax.axis_index("seq")
    m_me = lax.axis_index("mp")
    d_me = lax.axis_index("dp")
    count = counts[0]

    loads = [
        pltpu.make_async_copy(source, target, in_sem.at[at])
        for at, (source, target) in enumerate((
            (tokens_hbm, tokens), (gain_hbm, gain), (weight_hbm, weight),
            (grad_hbm, grad_out), (out_weight_hbm, out_weight),
        ))
    ]
    for load in loads:
        load.start()

    def peer(axis, me, size, step):
        return {axis: lax.rem(me + (step + size), size)}

    barrier = pltpu.get_barrier_semaphore()
    greeted = [("seq", s_me, n_seq, step) for step in sorted({2, n_seq - 2, 1, n_seq - 1})]
    greeted += [("dp", d_me, n_dp, step) for step in range(1, n_dp)]
    greeted += [("mp", m_me, n_mp, step) for step in range(1, n_mp)]
    for other in greeted:
        pl.semaphore_signal(barrier, inc=1, device_id=peer(*other), device_id_type=MESH)

    started = []

    def remote(src, dst, send, recv, device):
        return pltpu.make_async_remote_copy(
            src_ref=src, dst_ref=dst, send_sem=send, recv_sem=recv,
            device_id=device, device_id_type=MESH,
        )

    def go(copy):
        copy.start()
        started.append(copy)

    def position(shape, axis):
        at = iota(shape, axis)
        return 2 * (at % HALF) + at // HALF

    def head(h, part=0):
        return slice(part * GROUP + h * HDIM, part * GROUP + (h + 1) * HDIM)

    def far_at(h):
        return slice(h * HALF, (h + 1) * HALF)

    order = one_hot(position((BLOCK, BLOCK), 0) == iota((BLOCK, BLOCK), 1))
    eye = one_hot(iota((BLOCK, BLOCK), 0) == iota((BLOCK, BLOCK), 1))

    for load in loads[:3]:
        load.wait()
    x = dot_nn(order, tokens[...])
    mean = row_sum(x) * (1.0 / width)
    centered = x - mean
    inverse_std = lax.rsqrt(row_sum(centered * centered) * (1.0 / width) + 1e-05)
    normal_form = centered * inverse_std
    normed = (normal_form * gain[...].reshape(1, width)).astype(BF)
    normed_s[...] = normed
    kv_here[...] = dot_nt(weight[GROUP:, :], normed).astype(BF)
    for part in range(2):
        for h in range(2):
            kv_far[mid, head(h, part), :] = kv_here[head(h, part), far_at(h)]

    pl.semaphore_wait(barrier, len(greeted))

    def seq_peer(step):
        return peer("seq", s_me, n_seq, step)

    def gather_copy(which, stage, way, far, piece):
        blocks, send, recv = gathers[which]
        sign = 1 - 2 * way
        source, target = mid - sign * 2 * stage, mid - sign * (2 * stage + far)
        at = pl.ds(piece * GROUP, GROUP)
        return remote(
            blocks.at[source % n_seq, at], blocks.at[target % n_seq, at],
            send.at[stage, way, far - 1, piece], recv.at[stage, way, far - 1, piece],
            seq_peer(sign * far),
        )

    gathers = ((kv_far, kv_ss, kv_rs), (qd_far, qd_ss, qd_rs))

    def moves(stage):
        return [
            (stage, way, far, piece)
            for far in (2, 1) for piece in range(2) for way in range(2)
            if 2 * stage + far < mid or (2 * stage + far == mid and way == piece)
        ]

    def gather_stage(which, stage):
        for move in moves(stage):
            if move[2] == 2:
                gather_copy(which, *move).wait_recv()
                for later in (moves(stage + 1) if 2 * stage + 2 < mid else []):
                    if (later[1], later[3]) == (move[1], move[3]):
                        go(gather_copy(which, *later))
        for move in moves(stage):
            if move[2] == 1:
                gather_copy(which, *move).wait_recv()

    for move in moves(0):
        go(gather_copy(0, *move))
    qd_here[:GROUP, :] = dot_nt(weight[:GROUP, :], normed).astype(BF)
    for load in loads[3:]:
        load.wait()
    go_s[...] = dot_nn(order, grad_out[...]).astype(BF)
    qd_here[GROUP:, :] = dot_nt(out_weight[...], go_s[...]).astype(BF)
    for part in range(2):
        for h in range(2):
            qd_far[mid, head(h, part), :] = qd_here[head(h, part), far_at(h)]
    for move in moves(0):
        go(gather_copy(1, *move))

    live_key = s_me * BLOCK + position((1, BLOCK), 1) < count
    live_query = s_me * BLOCK + position((BLOCK, 1), 0) < count
    for h in range(2):
        q_rows[h] = dot_nt(eye, qd_here[head(h), :]).astype(BF)
        da_rows[h] = dot_nt(eye, qd_here[head(h, 1), :]).astype(BF)
        k_rows[h] = dot_nt(eye[:HALF, :HALF], kv_far[mid, head(h), :]).astype(BF)
        v_rows[h] = dot_nt(eye[:HALF, :HALF], kv_far[mid, head(h, 1), :]).astype(BF)
        near_scores[h] = jnp.where(
            live_key, dot_nn(q_rows[h], kv_here[head(h), :]) * scaling, far_below
        )
        near_probs[h] = dot_nn(da_rows[h], kv_here[head(h, 1), :])
        top[h] = jnp.maximum(
            near_scores[h, far_at(h), :HALF], near_scores[h, far_at(h), HALF:]
        )

    def far_scores(slot):
        owner = lax.rem(s_me + (slot - mid + n_seq), n_seq)
        for h in range(2):
            live = owner * BLOCK + 2 * iota((1, HALF), 1) + h < count
            score = dot_nn(q_rows[h, far_at(h), :], kv_far[slot, head(h), :]) * scaling
            score = jnp.where(live, score, far_below)
            scores[h, slot] = score
            top[h] = jnp.maximum(top[h], score)
            probs[h, slot] = dot_nn(da_rows[h, far_at(h), :], kv_far[slot, head(h, 1), :])

    def turned_scores(slot):
        for h in range(2):
            live = s_me * BLOCK + 2 * iota((HALF, 1), 0) + h < count
            score = dot_nn(k_rows[h], qd_far[slot, head(h), :]) * scaling
            scores_t[h, slot] = jnp.where(live, score, far_below)
            probs_t[h, slot] = dot_nn(v_rows[h], qd_far[slot, head(h, 1), :])

    place = iota((width, 1), 0).astype(F32)
    piece_at = floor_div(place, rows)
    dp_at = floor_div(piece_at, n_seq)
    feature = n_dp * rows * (piece_at - n_seq * dp_at) + rows * dp_at + (place - rows * piece_at)
    spread = one_hot(feature == iota((width, width), 1).astype(F32))

    def fill_pads():
        for m in range(n_mp):
            to, of = pl.ds(m * LANES, GROUP), slice(m * GROUP, (m + 1) * GROUP)
            rest = pl.ds(m * LANES + GROUP, LANES - GROUP)
            form_pad[:, to] = normal_form[:, of]
            form_pad[:, rest] = jnp.zeros((BLOCK, LANES - GROUP), F32)
            gain_pad[:, to] = gain[...].reshape(1, width)[:, of]
            gain_pad[:, rest] = jnp.zeros((1, LANES - GROUP), F32)

    def fill_normed():
        normed_p[...] = dot_nt(spread, normed_s[...]).astype(BF)

    def fill_go():
        go_p[...] = dot_nt(spread, go_s[...]).astype(BF)

    def fill_weight():
        for m in range(n_mp):
            weight_pad[:, m * LANES : m * LANES + GROUP] = weight[:, m * GROUP : (m + 1) * GROUP]
            weight_pad[:, m * LANES + GROUP : (m + 1) * LANES] = jnp.zeros(
                (3 * GROUP, LANES - GROUP), BF
            )

    def fill_own():
        mine = one_hot(
            (iota((width, LANES), 0) == m_me * GROUP + iota((width, LANES), 1))
            & (iota((width, LANES), 1) < GROUP)
        )
        own_parts[0] = dot_nn(go_s[...], mine)
        for part in range(4):
            d_parts[part, GROUP:, :] = jnp.zeros((LANES - GROUP, BLOCK), BF)

    fillers = [fill_pads, fill_normed, fill_go, fill_weight, fill_own]

    def stage_slots(stage):
        aways = (2 * stage + 1, 2 * stage + 2)
        return [mid - away for away in aways] + [mid + away for away in aways if away < mid]

    far_scores(mid)
    turned_scores(mid)
    stages = n_seq // 4
    for stage in range(stages):
        gather_stage(0, stage)
        if stage + 1 < stages:
            gather_stage(1, stage)
        for slot in stage_slots(stage):
            far_scores(slot)
        if stage + 1 < stages:
            for slot in stage_slots(stage):
                turned_scores(slot)
            for _ in range(2):
                if fillers:
                    fillers.pop(0)()
    for filler in fillers:
        filler()

    inverse_total, deltas = [], []
    lane = iota((HALF, LANES), 1)
    stats = jnp.zeros((HALF, LANES), F32)
    for h in range(2):
        far_top = jnp.max(top[h], axis=1, keepdims=True)
        total = jnp.zeros((HALF, HALF), F32)
        delta = jnp.zeros((HALF, HALF), F32)
        for slot in range(n_seq):
            grown = jnp.exp(scores[h, slot] - far_top)
            scores[h, slot] = grown
            total = total + grown
            delta = delta + grown * probs[h, slot]
        halves_total, halves_delta = [], []
        for half in range(2):
            at = far_at(half)
            near = near_scores[h, at, :]
            peak = far_top if half == h else jnp.max(near, axis=1, keepdims=True)
            grown = jnp.exp(near - peak)
            near_scores[h, at, :] = grown
            sums = row_sum(grown)
            mixed = row_sum(grown * near_probs[h, at, :])
            if half == h:
                sums = sums + row_sum(total)
                mixed = mixed + row_sum(delta)
            inverse = jnp.where(live_query[at, :], 1.0 / sums, 0.0)
            halves_total.append(inverse)
            halves_delta.append(mixed * inverse)
        inverse_total.append(halves_total)
        deltas.append(halves_delta)
        for at, value in enumerate((far_top, halves_total[h], halves_delta[h])):
            stats = jnp.where(lane == 3 * h + at, value, stats)
    stat_send[...] = jnp.transpose(stats)[:8, :]

    def stat_copy(step):
        return remote(
            stat_send, stat_recv.at[step - 1], st_ss.at[step - 1], st_rs.at[step - 1], seq_peer(step)
        )

    far_first = sorted(range(1, n_seq), key=lambda step: -min(step, n_seq - step))
    for step in far_first:
        go(stat_copy(step))

    attended = [jnp.zeros((HDIM, HALF), F32) for _ in range(2)]
    d_query = [jnp.zeros((HDIM, HALF), F32) for _ in range(2)]

    def far_terms(slot):
        for h in range(2):
            weights = scores[h, slot] * inverse_total[h][h]
            ds = (weights * (probs[h, slot] - deltas[h][h]) * scaling).astype(BF)
            attended[h] = attended[h] + dot_nt(kv_far[slot, head(h, 1), :], weights.astype(BF))
            d_query[h] = d_query[h] + dot_nt(kv_far[slot, head(h), :], ds)

    near_terms = []

    def near_part():
        for h in range(2):
            weights = near_scores[h] * jnp.concatenate(inverse_total[h], axis=0)
            bar = weights.astype(BF)
            delta = jnp.concatenate(deltas[h], axis=0)
            ds = (weights * (near_probs[h] - delta) * scaling).astype(BF)
            near_terms.append((dot_nn(qd_here[head(h), :], ds), dot_nn(qd_here[head(h, 1), :], bar)))
            near_att = dot_nt(kv_here[head(h, 1), :], bar)
            near_dq = dot_nt(kv_here[head(h), :], ds)
            for half in range(2):
                at = far_at(half)
                att, dq = near_att[:, at], near_dq[:, at]
                if half == h:
                    att, dq = att + attended[h], dq + d_query[h]
                d_parts[0, head(h), at] = att.astype(BF)
                d_parts[1, head(h), at] = dq.astype(BF)

    def y_copy(phase, step):
        to = lax.rem(d_me + step, n_dp)
        at = pl.ds(pl.multiple_of(to * chunk, 16), chunk)
        return remote(
            y_send.at[phase, at], y_recv.at[phase, step - 1],
            y_ss.at[phase, step - 1], y_rs.at[phase, step - 1], {"dp": to},
        )

    def z_copy(phase, step):
        to = lax.rem(s_me + step, n_seq)
        at = pl.ds(pl.multiple_of(to * rows_pad, 16), rows_pad)
        return remote(
            z_send.at[phase, at], z_recv.at[phase, step - 1],
            z_ss.at[phase, step - 1], z_rs.at[phase, step - 1], {"seq": to},
        )

    def y_start(phase, sides):
        for side, (left_side, part) in enumerate(sides):
            y_send[phase, :, side * LANES : (side + 1) * LANES] = dot_nt(
                left_side[...], d_parts[part]
            ).astype(BF)
        for step in range(1, n_dp):
            go(y_copy(phase, step))

    widen = one_hot(
        (iota((n_seq * rows_pad, chunk), 0) // rows_pad * rows
         + iota((n_seq * rows_pad, chunk), 0) % rows_pad == iota((n_seq * rows_pad, chunk), 1))
        & (iota((n_seq * rows_pad, chunk), 0) % rows_pad < rows)
    )

    def z_start(phase):
        mine = pl.ds(pl.multiple_of(d_me * chunk, 16), chunk)
        total = y_send[phase, mine, :].astype(F32)
        for step in range(1, n_dp):
            y_copy(phase, step).wait_recv()
            total = total + y_recv[phase, step - 1].astype(F32)
        z_send[phase] = dot_nn(widen, total.astype(BF)).astype(BF)
        for step in far_first:
            go(z_copy(phase, step))

    def z_end(phase, result):
        mine = pl.ds(pl.multiple_of(s_me * rows_pad, 16), rows_pad)
        total = z_send[phase, mine, :].astype(F32)
        for step in far_first[::-1]:
            z_copy(phase, step).wait_recv()
            total = total + z_recv[phase, step - 1].astype(F32)
        result[...] = total

    for slot in range(n_seq):
        far_terms(slot)
    near_part()
    y_start(0, ((go_p, 0), (normed_p, 1)))
    gather_stage(1, stages - 1)
    for slot in stage_slots(stages - 1):
        turned_scores(slot)

    far_dk = [jnp.zeros((HDIM, HALF), F32) for _ in range(2)]
    far_dv = [jnp.zeros((HDIM, HALF), F32) for _ in range(2)]

    def key_terms(slot, stat):
        for h in range(2):
            weights = jnp.exp(scores_t[h, slot] - stat[3 * h : 3 * h + 1, :]) * stat[3 * h + 1 : 3 * h + 2, :]
            ds = (weights * (probs_t[h, slot] - stat[3 * h + 2 : 3 * h + 3, :]) * scaling).astype(BF)
            far_dk[h] = far_dk[h] + dot_nt(qd_far[slot, head(h), :], ds)
            far_dv[h] = far_dv[h] + dot_nt(qd_far[slot, head(h, 1), :], weights.astype(BF))

    key_terms(mid, stat_send[...])
    near_first = far_first[::-1]
    for at, step in enumerate(near_first):
        if at == len(near_first) // 2:
            z_start(0)
        stat_copy(step).wait_recv()
        key_terms((mid - step) % n_seq, stat_recv[step - 1])
    for h in range(2):
        for part, far_part in ((0, far_dk), (1, far_dv)):
            for half in range(2):
                term = near_terms[h][part][:, far_at(half)]
                if half == h:
                    term = term + far_part[h]
                d_parts[2 + part, head(h), far_at(half)] = term.astype(BF)

    y_start(1, ((normed_p, 2), (normed_p, 3)))
    d_rows = jnp.zeros((BLOCK, n_mp * LANES), F32)
    for part in range(3):
        d_part = dot_nt(eye, d_parts[1 + part, :GROUP, :]).astype(BF)
        d_rows = d_rows + dot_nn(d_part, weight_pad[part * GROUP : (part + 1) * GROUP, :])
    d_rows = d_rows.astype(BF).astype(F32)
    gain_terms = jnp.sum(d_rows * form_pad[...], axis=0, keepdims=True)
    for m in range(n_mp):
        gm_send[m] = jnp.broadcast_to(gain_terms[:, m * LANES : (m + 1) * LANES], (8, LANES))

    def gm_copy(step):
        to = lax.rem(m_me + step, n_mp)
        return remote(
            gm_send.at[to], gm_recv.at[step - 1], gm_ss.at[step - 1], gm_rs.at[step - 1], {"mp": to}
        )

    def gy_copy(step):
        return remote(
            gy_send, gy_recv.at[step - 1], gy_ss.at[step - 1], gy_rs.at[step - 1],
            peer("dp", d_me, n_dp, step),
        )

    def gz_copy(step):
        return remote(
            gz_send, gz_recv.at[step - 1], gz_ss.at[step - 1], gz_rs.at[step - 1], seq_peer(step)
        )

    for step in range(1, n_mp):
        go(gm_copy(step))
    scaled_rows = d_rows * gain_pad[...]
    first = row_sum(scaled_rows)
    second = row_sum(scaled_rows * form_pad[...])
    lane = iota((BLOCK, LANES), 1)
    extra = jnp.zeros((BLOCK, LANES), F32)
    for at, value in ((GROUP, first), (GROUP + 2, second)):
        coarse = value.astype(BF).astype(F32)
        extra = jnp.where(lane == at, coarse, extra)
        extra = jnp.where(lane == at + 1, value - coarse, extra)
    for m in range(n_mp):
        mp_send[m] = (d_rows[:, m * LANES : (m + 1) * LANES] + extra).astype(BF)

    def mp_copy(step):
        to = lax.rem(m_me + step, n_mp)
        return remote(
            mp_send.at[to], mp_recv.at[step - 1], mp_ss.at[step - 1], mp_rs.at[step - 1], {"mp": to}
        )

    for step in range(1, n_mp):
        go(mp_copy(step))
    gain_total = gm_send[m_me]
    for step in range(1, n_mp):
        gm_copy(step).wait_recv()
        gain_total = gain_total + gm_recv[step - 1]
    gy_send[...] = gain_total
    for step in range(1, n_dp):
        go(gy_copy(step))
    z_start(1)
    for step in range(1, n_dp):
        gy_copy(step).wait_recv()
        gain_total = gain_total + gy_recv[step - 1]
    gz_send[...] = gain_total
    for step in far_first:
        go(gz_copy(step))

    d_normed = mp_send[m_me].astype(F32)
    for step in range(1, n_mp):
        mp_copy(step).wait_recv()
        d_normed = d_normed + mp_recv[step - 1].astype(F32)
    own = pl.ds(pl.multiple_of(m_me * LANES, LANES), LANES)
    form = form_pad[:, own]
    mean_scaled = (d_normed[:, GROUP : GROUP + 1] + d_normed[:, GROUP + 1 : GROUP + 2]) * (1.0 / width)
    mean_mixed = (d_normed[:, GROUP + 2 : GROUP + 3] + d_normed[:, GROUP + 3 : GROUP + 4]) * (1.0 / width)
    scaled = d_normed * gain_pad[:, own]
    d_tok = own_parts[0] + (scaled - mean_scaled - form * mean_mixed) * inverse_std
    turned = dot_nt(eye[:LANES, :LANES], d_tok.astype(BF)).astype(BF)
    tok_out[...] = dot_nn(turned, order).astype(BF)[:GROUP, :]
    z_end(0, early_out)
    z_end(1, late_out)
    for step in far_first[::-1]:
        gz_copy(step).wait_recv()
        gain_total = gain_total + gz_recv[step - 1]
    gain_out[...] = gain_total
    for copy in started:
        copy.wait_send()


def per_device(n_seq, n_mp, n_dp, tokens, gain, qkv_weight, out_weight, counts, grad_out):
    width = n_mp * GROUP
    chunk = width // n_dp
    rows = chunk // n_seq
    rows_pad = -(-rows // 16) * 16
    mid = n_seq // 2
    weight = qkv_weight.transpose(1, 2, 0).reshape(3 * GROUP, width)
    vmem = pl.BlockSpec(memory_space=pltpu.VMEM)
    dma = pltpu.SemaphoreType.DMA
    far_block = pltpu.VMEM((n_seq, 2 * GROUP, HALF), BF)
    far_square = pltpu.VMEM((2, n_seq, HALF, HALF), F32)
    scratch = [
        pltpu.VMEM((BLOCK, width), BF),
        pltpu.VMEM((BLOCK, width), BF),
        pltpu.VMEM((width,), F32),
        pltpu.VMEM((3 * GROUP, width), BF),
        pltpu.VMEM((GROUP, width), BF),
        far_block, far_block, far_square, far_square, far_square, far_square,
        pltpu.VMEM((2, HALF, HALF), F32),
        pltpu.VMEM((2 * GROUP, BLOCK), BF),
        pltpu.VMEM((2 * GROUP, BLOCK), BF),
        pltpu.VMEM((2, BLOCK, HDIM), BF),
        pltpu.VMEM((2, BLOCK, HDIM), BF),
        pltpu.VMEM((2, HALF, HDIM), BF),
        pltpu.VMEM((2, HALF, HDIM), BF),
        pltpu.VMEM((2, BLOCK, BLOCK), F32),
        pltpu.VMEM((2, BLOCK, BLOCK), F32),
        pltpu.VMEM((BLOCK, width), BF),
        pltpu.VMEM((BLOCK, width), BF),
        pltpu.VMEM((width, BLOCK), BF),
        pltpu.VMEM((width, BLOCK), BF),
        pltpu.VMEM((1, n_mp * LANES), F32),
        pltpu.VMEM((BLOCK, n_mp * LANES), F32),
        pltpu.VMEM((3 * GROUP, n_mp * LANES), BF),
        pltpu.VMEM((4, LANES, BLOCK), BF),
        pltpu.VMEM((1, BLOCK, LANES), F32),
        pltpu.VMEM((8, LANES), F32),
        pltpu.VMEM((n_seq - 1, 8, LANES), F32),
        pltpu.VMEM((2, width, 2 * LANES), BF),
        pltpu.VMEM((2, n_dp - 1, chunk, 2 * LANES), BF),
        pltpu.VMEM((2, n_seq * rows_pad, 2 * LANES), BF),
        pltpu.VMEM((2, n_seq - 1, rows_pad, 2 * LANES), BF),
        pltpu.VMEM((n_mp, BLOCK, LANES), BF),
        pltpu.VMEM((n_mp - 1, BLOCK, LANES), BF),
        pltpu.VMEM((n_mp, 8, LANES), F32),
        pltpu.VMEM((n_mp - 1, 8, LANES), F32),
        pltpu.VMEM((8, LANES), F32),
        pltpu.VMEM((n_dp - 1, 8, LANES), F32),
        pltpu.VMEM((8, LANES), F32),
        pltpu.VMEM((n_seq - 1, 8, LANES), F32),
        dma((5,)),
    ]
    for shape in (
        (n_seq // 4, 2, 2, 2), (n_seq // 4, 2, 2, 2), (n_seq - 1,), (2, n_dp - 1), (2, n_seq - 1), (n_mp - 1,),
        (n_mp - 1,), (n_dp - 1,), (n_seq - 1,),
    ):
        scratch += [dma(shape), dma(shape)]
    d_tok, early, late, d_gain = pl.pallas_call(
        functools.partial(layer_kernel, n_seq, n_mp, n_dp),
        out_shape=(
            jax.ShapeDtypeStruct((GROUP, BLOCK), BF),
            jax.ShapeDtypeStruct((rows_pad, 2 * LANES), F32),
            jax.ShapeDtypeStruct((rows_pad, 2 * LANES), F32),
            jax.ShapeDtypeStruct((8, LANES), F32),
        ),
        in_specs=[pl.BlockSpec(memory_space=pltpu.SMEM)] + [pl.BlockSpec(memory_space=pl.ANY)] * 5,
        out_specs=(vmem,) * 4,
        scratch_shapes=scratch,
        compiler_params=pltpu.CompilerParams(
            collective_id=0, has_side_effects=True, vmem_limit_bytes=VMEM_BYTES
        ),
    )(counts, tokens[0], grad_out[0], gain, weight, out_weight)
    tok_turned, d_qkv, out_turned, gain_total = pl.pallas_call(
        functools.partial(shape_results, rows),
        out_shape=(
            jax.ShapeDtypeStruct((GROUP, BLOCK), BF),
            jax.ShapeDtypeStruct((rows, 3, GROUP), F32),
            jax.ShapeDtypeStruct((rows, GROUP), F32),
            jax.ShapeDtypeStruct((GROUP,), F32),
        ),
        in_specs=[vmem] * 4,
        out_specs=(vmem,) * 4,
        compiler_params=pltpu.CompilerParams(vmem_limit_bytes=VMEM_BYTES),
    )(d_tok, early, late, d_gain)
    return (tok_turned.T[None], d_qkv, out_turned.T, gain_total)


def shape_results(rows, d_tok, early, late, d_gain, tok_out, qkv_out, out_out, gain_out):
    tok_out[...] = d_tok[...]
    qkv_out[:, 0, :] = early[:rows, LANES : LANES + GROUP]
    qkv_out[:, 1, :] = late[:rows, :GROUP]
    qkv_out[:, 2, :] = late[:rows, LANES : LANES + GROUP]
    out_out[...] = early[:rows, :GROUP]
    gain_out[...] = d_gain[0, :GROUP]


def solution(mesh):
    sizes = (mesh.shape["seq"], mesh.shape["mp"], mesh.shape["dp"])
    placed = (
        P("dp", "seq", None),
        P(),
        P(None, None, "mp"),
        P("mp", None),
        P("dp"),
        P("dp", "seq", None),
    )
    return jax.shard_map(
        functools.partial(per_device, *sizes),
        mesh=mesh,
        in_specs=placed,
        out_specs=(
            P("dp", "seq", "mp"),
            P(("seq", "dp"), None, "mp"),
            P("mp", ("seq", "dp")),
            P("mp"),
        ),
        check_vma=False,
    )
```

```python
import functools
import math

import jax
import jax.numpy as jnp
from jax import lax
from jax.experimental import pallas as pl
from jax.experimental.pallas import tpu as pltpu
from jax.sharding import PartitionSpec as P

HDIM = 48
BLOCK = 256
HALF = BLOCK // 2
GROUP = 2 * HDIM
LANES = 128
VMEM_BYTES = 60 * 1024 * 1024
MESH = pl.DeviceIdType.MESH
BF = jnp.bfloat16
F32 = jnp.float32
far_below = -1e30


def dot_nn(left, right):
    return lax.dot_general(left, right, (((1,), (0,)), ((), ())), preferred_element_type=F32)


def dot_nt(left, right):
    return lax.dot_general(left, right, (((1,), (1,)), ((), ())), preferred_element_type=F32)


def iota(shape, axis):
    return lax.broadcasted_iota(jnp.int32, shape, axis)


def one_hot(condition):
    return jnp.where(condition, 1.0, 0.0).astype(BF)


def row_sum(value):
    return jnp.sum(value, axis=1, keepdims=True)


def floor_div(value, by):
    return jnp.floor((value + 0.5) * (1.0 / by))


def layer_kernel(
    n_seq, n_mp, n_dp,
    counts, tokens_hbm, grad_hbm, gain_hbm, weight_hbm, out_weight_hbm,
    tok_out, qkv_out, out_out, gain_out,
    tokens, grad_out, gain, weight, out_weight,
    kv_far, qd_far, scores, probs, scores_t, probs_t, top, kv_here, qd_here, q_rows, da_rows, k_rows, v_rows,
    near_scores, near_probs, normed_s, go_s, normed_p, go_p, gain_pad, form_pad, weight_pad,
    d_parts, own_parts, stat_send, stat_recv,
    side_recv, y_recv, z_send, z_recv, mp_send, mp_recv,
    gm_send, gm_recv, gy_send, gy_recv,
    in_sem, kv_ss, kv_rs, qd_ss, qd_rs, st_ss, st_rs, sd_ss, sd_rs, y_ss, y_rs, z_ss, z_rs, mp_ss, mp_rs,
    gm_ss, gm_rs, gy_ss, gy_rs,
):
    width = n_mp * GROUP
    chunk = width // n_dp
    rows = chunk // n_seq
    rows_pad = -(-rows // 16) * 16
    mid = n_seq // 2
    scaling = 1.0 / math.sqrt(HDIM)
    s_me = lax.axis_index("seq")
    m_me = lax.axis_index("mp")
    d_me = lax.axis_index("dp")
    count = counts[0]

    loads = [
        pltpu.make_async_copy(source, target, in_sem.at[at])
        for at, (source, target) in enumerate((
            (tokens_hbm, tokens), (gain_hbm, gain), (weight_hbm, weight),
            (grad_hbm, grad_out), (out_weight_hbm, out_weight),
        ))
    ]
    for load in loads:
        load.start()

    def peer(axis, me, size, step):
        return {axis: lax.rem(me + (step + size), size)}

    barrier = pltpu.get_barrier_semaphore()
    greeted = [("seq", s_me, n_seq, step) for step in sorted({2, n_seq - 2, 1, n_seq - 1})]
    greeted += [("dp", d_me, n_dp, step) for step in range(1, n_dp)]
    greeted += [("mp", m_me, n_mp, step) for step in range(1, n_mp)]
    for other in greeted:
        pl.semaphore_signal(barrier, inc=1, device_id=peer(*other), device_id_type=MESH)

    started = []

    def remote(src, dst, send, recv, device):
        return pltpu.make_async_remote_copy(
            src_ref=src, dst_ref=dst, send_sem=send, recv_sem=recv,
            device_id=device, device_id_type=MESH,
        )

    def go(copy):
        copy.start()
        started.append(copy)

    def position(shape, axis):
        at = iota(shape, axis)
        return 2 * (at % HALF) + at // HALF

    def head(h, part=0):
        return slice(part * GROUP + h * HDIM, part * GROUP + (h + 1) * HDIM)

    def far_at(h):
        return slice(h * HALF, (h + 1) * HALF)

    order = one_hot(position((BLOCK, BLOCK), 0) == iota((BLOCK, BLOCK), 1))
    eye = one_hot(iota((BLOCK, BLOCK), 0) == iota((BLOCK, BLOCK), 1))

    loads[0].wait()
    x = dot_nn(order, tokens[...])
    mean = row_sum(x) * (1.0 / width)
    centered = x - mean
    inverse_std = lax.rsqrt(row_sum(centered * centered) * (1.0 / width) + 1e-05)
    normal_form = centered * inverse_std
    loads[1].wait()
    normed = (normal_form * gain[...].reshape(1, width)).astype(BF)
    normed_s[...] = normed
    loads[2].wait()
    kv_here[...] = dot_nt(weight[GROUP:, :], normed).astype(BF)
    for part in range(2):
        for h in range(2):
            kv_far[mid, head(h, part), :] = kv_here[head(h, part), far_at(h)]

    pl.semaphore_wait(barrier, len(greeted))

    def seq_peer(step):
        return peer("seq", s_me, n_seq, step)

    def gather_copy(which, stage, way, far, piece):
        blocks, send, recv = gathers[which]
        sign = 1 - 2 * way
        source, target = mid - sign * 2 * stage, mid - sign * (2 * stage + far)
        at = pl.ds(piece * GROUP, GROUP)
        return remote(
            blocks.at[source % n_seq, at], blocks.at[target % n_seq, at],
            send.at[stage, way, far - 1, piece], recv.at[stage, way, far - 1, piece],
            seq_peer(sign * far),
        )

    gathers = ((kv_far, kv_ss, kv_rs), (qd_far, qd_ss, qd_rs))

    def moves(stage):
        return [
            (stage, way, far, piece)
            for far in (2, 1) for piece in range(2) for way in range(2)
            if 2 * stage + far < mid or (2 * stage + far == mid and way == piece)
        ]

    def gather_stage(which, stage):
        for move in moves(stage):
            if move[2] == 2:
                gather_copy(which, *move).wait_recv()
                for later in (moves(stage + 1) if 2 * stage + 2 < mid else []):
                    if (later[1], later[3]) == (move[1], move[3]):
                        go(gather_copy(which, *later))
        for move in moves(stage):
            if move[2] == 1:
                gather_copy(which, *move).wait_recv()

    for move in moves(0):
        go(gather_copy(0, *move))
    qd_here[:GROUP, :] = dot_nt(weight[:GROUP, :], normed).astype(BF)
    for load in loads[3:]:
        load.wait()
    go_s[...] = dot_nn(order, grad_out[...]).astype(BF)
    qd_here[GROUP:, :] = dot_nt(out_weight[...], go_s[...]).astype(BF)
    for part in range(2):
        for h in range(2):
            qd_far[mid, head(h, part), :] = qd_here[head(h, part), far_at(h)]
    for move in moves(0):
        go(gather_copy(1, *move))

    live_key = s_me * BLOCK + position((1, BLOCK), 1) < count
    live_query = s_me * BLOCK + position((BLOCK, 1), 0) < count
    for h in range(2):
        q_rows[h] = dot_nt(eye, qd_here[head(h), :]).astype(BF)
        da_rows[h] = dot_nt(eye, qd_here[head(h, 1), :]).astype(BF)
        k_rows[h] = dot_nt(eye[:HALF, :HALF], kv_far[mid, head(h), :]).astype(BF)
        v_rows[h] = dot_nt(eye[:HALF, :HALF], kv_far[mid, head(h, 1), :]).astype(BF)
        near_scores[h] = jnp.where(
            live_key, dot_nn(q_rows[h], kv_here[head(h), :]) * scaling, far_below
        )
        near_probs[h] = dot_nn(da_rows[h], kv_here[head(h, 1), :])
        top[h] = jnp.maximum(
            near_scores[h, far_at(h), :HALF], near_scores[h, far_at(h), HALF:]
        )

    def far_scores(slot):
        owner = lax.rem(s_me + (slot - mid + n_seq), n_seq)
        for h in range(2):
            live = owner * BLOCK + 2 * iota((1, HALF), 1) + h < count
            score = dot_nn(q_rows[h, far_at(h), :], kv_far[slot, head(h), :]) * scaling
            score = jnp.where(live, score, far_below)
            scores[h, slot] = score
            top[h] = jnp.maximum(top[h], score)
            probs[h, slot] = dot_nn(da_rows[h, far_at(h), :], kv_far[slot, head(h, 1), :])

    def turned_scores(slot):
        for h in range(2):
            live = s_me * BLOCK + 2 * iota((HALF, 1), 0) + h < count
            score = dot_nn(k_rows[h], qd_far[slot, head(h), :]) * scaling
            scores_t[h, slot] = jnp.where(live, score, far_below)
            probs_t[h, slot] = dot_nn(v_rows[h], qd_far[slot, head(h, 1), :])

    place = iota((width, 1), 0).astype(F32)
    piece_at = floor_div(place, rows)
    dp_at = floor_div(piece_at, n_seq)
    feature = n_dp * rows * (piece_at - n_seq * dp_at) + rows * dp_at + (place - rows * piece_at)
    spread = one_hot(feature == iota((width, width), 1).astype(F32))

    def fill_pads():
        for m in range(n_mp):
            to, of = pl.ds(m * LANES, GROUP), slice(m * GROUP, (m + 1) * GROUP)
            rest = pl.ds(m * LANES + GROUP, LANES - GROUP)
            form_pad[:, to] = normal_form[:, of]
            form_pad[:, rest] = jnp.zeros((BLOCK, LANES - GROUP), F32)
            gain_pad[:, to] = gain[...].reshape(1, width)[:, of]
            gain_pad[:, rest] = jnp.zeros((1, LANES - GROUP), F32)

    def chunk_of(device):
        return pl.ds(pl.multiple_of(device * chunk, 16), chunk)

    def side_copy(side, step):
        to = lax.rem(d_me + step, n_dp)
        return remote(
            (go_p, normed_p)[side].at[chunk_of(to)], side_recv.at[side, step - 1],
            sd_ss.at[side, step - 1], sd_rs.at[side, step - 1], {"dp": to},
        )

    def fill_normed():
        normed_p[...] = dot_nt(spread, normed_s[...]).astype(BF)
        for step in range(1, n_dp):
            go(side_copy(1, step))

    def fill_go():
        go_p[...] = dot_nt(spread, go_s[...]).astype(BF)
        for step in range(1, n_dp):
            go(side_copy(0, step))

    def fill_weight():
        for m in range(n_mp):
            weight_pad[:, m * LANES : m * LANES + GROUP] = weight[:, m * GROUP : (m + 1) * GROUP]
            weight_pad[:, m * LANES + GROUP : (m + 1) * LANES] = jnp.zeros(
                (3 * GROUP, LANES - GROUP), BF
            )

    def fill_own():
        mine = one_hot(
            (iota((width, LANES), 0) == m_me * GROUP + iota((width, LANES), 1))
            & (iota((width, LANES), 1) < GROUP)
        )
        own_parts[0] = dot_nn(go_s[...], mine)
        z_send[...] = jnp.zeros(z_send.shape, BF)

    fillers = [fill_pads, fill_normed, fill_go, fill_weight, fill_own]

    def stage_slots(stage):
        aways = (2 * stage + 1, 2 * stage + 2)
        return [mid - away for away in aways] + [mid + away for away in aways if away < mid]

    far_scores(mid)
    turned_scores(mid)
    stages = n_seq // 4
    lag = min(1, stages - 1)
    done = [mid]
    for stage in range(stages - 1):
        gather_stage(0, stage)
        if stage >= lag:
            gather_stage(1, stage - lag)
        for slot in stage_slots(stage):
            far_scores(slot)
            done.append(slot)
        if stage >= lag:
            for slot in stage_slots(stage - lag):
                turned_scores(slot)
        for _ in range(2):
            if fillers:
                fillers.pop(0)()
    for filler in fillers:
        filler()

    def grow(h, slots, peak):
        total = jnp.zeros((HALF, HALF), F32)
        delta = jnp.zeros((HALF, HALF), F32)
        for slot in slots:
            grown = jnp.exp(scores[h, slot] - peak)
            scores[h, slot] = grown
            total = total + grown
            delta = delta + grown * probs[h, slot]
        return row_sum(total), row_sum(delta)

    first_peaks, first_sums = [], []
    for h in range(2):
        peaks, sums = [], []
        for half in range(2):
            at = far_at(half)
            near = near_scores[h, at, :]
            peak = jnp.max(top[h] if half == h else near, axis=1, keepdims=True)
            grown = jnp.exp(near - peak)
            near_scores[h, at, :] = grown
            total, delta = row_sum(grown), row_sum(grown * near_probs[h, at, :])
            if half == h:
                far_total, far_delta = grow(h, done, peak)
                total, delta = total + far_total, delta + far_delta
            peaks.append(peak)
            sums.append((total, delta))
        first_peaks.append(peaks)
        first_sums.append(sums)

    gather_stage(0, stages - 1)
    last = stage_slots(stages - 1)
    for slot in last:
        far_scores(slot)
    inverse_total, inverse_first, deltas = [], [], []
    lane = iota((HALF, LANES), 1)
    stats = jnp.zeros((HALF, LANES), F32)
    for h in range(2):
        far_top = jnp.max(top[h], axis=1, keepdims=True)
        shrink = jnp.exp(first_peaks[h][h] - far_top)
        last_total, last_delta = grow(h, last, far_top)
        total, delta = first_sums[h][h]
        inverse = jnp.where(
            live_query[far_at(h), :], 1.0 / (total * shrink + last_total), 0.0
        )
        far_delta = (delta * shrink + last_delta) * inverse
        total, delta = first_sums[h][1 - h]
        other = jnp.where(live_query[far_at(1 - h), :], 1.0 / total, 0.0)
        pairs = [(shrink * inverse, far_delta), (other, delta * other)]
        inverse_total.append(inverse)
        inverse_first.append([pairs[half != h][0] for half in range(2)])
        deltas.append([pairs[half != h][1] for half in range(2)])
        for at, value in enumerate((far_top, inverse, far_delta)):
            stats = jnp.where(lane == 3 * h + at, value, stats)
    stat_send[...] = jnp.transpose(stats)[:8, :]

    def stat_copy(step):
        return remote(
            stat_send, stat_recv.at[step - 1], st_ss.at[step - 1], st_rs.at[step - 1], seq_peer(step)
        )

    far_first = sorted(range(1, n_seq), key=lambda step: -min(step, n_seq - step))
    for step in far_first:
        go(stat_copy(step))

    attended = [jnp.zeros((HDIM, HALF), F32) for _ in range(2)]
    d_query = [jnp.zeros((HDIM, HALF), F32) for _ in range(2)]

    def far_terms(slot):
        for h in range(2):
            weights = scores[h, slot] * (inverse_total[h] if slot in last else inverse_first[h][h])
            ds = (weights * (probs[h, slot] - deltas[h][h]) * scaling).astype(BF)
            attended[h] = attended[h] + dot_nt(kv_far[slot, head(h, 1), :], weights.astype(BF))
            d_query[h] = d_query[h] + dot_nt(kv_far[slot, head(h), :], ds)

    near_terms = []

    def near_part():
        for h in range(2):
            weights = near_scores[h] * jnp.concatenate(inverse_first[h], axis=0)
            bar = weights.astype(BF)
            delta = jnp.concatenate(deltas[h], axis=0)
            ds = (weights * (near_probs[h] - delta) * scaling).astype(BF)
            near_terms.append((dot_nn(qd_here[head(h), :], ds), dot_nn(qd_here[head(h, 1), :], bar)))
            near_att = dot_nt(kv_here[head(h, 1), :], bar)
            near_dq = dot_nt(kv_here[head(h), :], ds)
            for half in range(2):
                at = far_at(half)
                att, dq = near_att[:, at], near_dq[:, at]
                if half == h:
                    att, dq = att + attended[h], dq + d_query[h]
                d_parts[0, head(h), at] = att.astype(BF)
                d_parts[1, head(h), at] = dq.astype(BF)

    def y_copy(phase, step):
        return remote(
            d_parts.at[pl.ds(2 * phase, 2)], y_recv.at[phase, step - 1],
            y_ss.at[phase, step - 1], y_rs.at[phase, step - 1], peer("dp", d_me, n_dp, step),
        )

    def z_copy(phase, step):
        to = lax.rem(s_me + step, n_seq)
        at = pl.ds(pl.multiple_of(to * rows_pad, 16), rows_pad)
        return remote(
            z_send.at[phase, at], z_recv.at[phase, step - 1],
            z_ss.at[phase, step - 1], z_rs.at[phase, step - 1], {"seq": to},
        )

    def y_start(phase):
        for step in range(1, n_dp):
            go(y_copy(phase, step))

    widen = one_hot(
        (iota((n_seq * rows_pad, chunk), 0) // rows_pad * rows
         + iota((n_seq * rows_pad, chunk), 0) % rows_pad == iota((n_seq * rows_pad, chunk), 1))
        & (iota((n_seq * rows_pad, chunk), 0) % rows_pad < rows)
    )

    def z_start(phase):
        mine = chunk_of(d_me)
        sides = ((go_p, 0), (normed_p, 1)) if phase == 0 else ((normed_p, 1), (normed_p, 1))
        if phase == 0:
            for side in range(2):
                for step in range(1, n_dp):
                    side_copy(side, step).wait_recv()
        sums = [dot_nt(side[mine, :], d_parts[2 * phase + at]) for at, (side, _) in enumerate(sides)]
        for step in range(1, n_dp):
            y_copy(phase, step).wait_recv()
            for at, (_, side) in enumerate(sides):
                sums[at] = sums[at] + dot_nt(side_recv[side, step - 1], y_recv[phase, step - 1, at])
        for at in range(2):
            z_send[phase, :, at * LANES : at * LANES + GROUP] = dot_nn(
                widen, sums[at].astype(BF)
            ).astype(BF)

    def z_go(phase):
        for step in far_first:
            go(z_copy(phase, step))

    def z_end(phase):
        mine = pl.ds(pl.multiple_of(s_me * rows_pad, 16), rows_pad)
        total = z_send[phase, mine, :].astype(F32)
        for step in far_first[::-1]:
            z_copy(phase, step).wait_recv()
            total = total + z_recv[phase, step - 1].astype(F32)
        return total

    waiting = list(range(stages - 1 - lag, stages))
    if stages > 1:
        gather_stage(1, waiting[0])
    for slot in done:
        far_terms(slot)
    if stages > 1:
        for slot in stage_slots(waiting.pop(0)):
            turned_scores(slot)
    for stage in waiting:
        gather_stage(1, stage)
    for slot in last:
        far_terms(slot)
    near_part()
    y_start(0)
    for stage in waiting:
        for slot in stage_slots(stage):
            turned_scores(slot)

    far_dk = [jnp.zeros((HDIM, HALF), F32) for _ in range(2)]
    far_dv = [jnp.zeros((HDIM, HALF), F32) for _ in range(2)]

    def key_terms(slot, stat):
        for h in range(2):
            weights = jnp.exp(scores_t[h, slot] - stat[3 * h : 3 * h + 1, :]) * stat[3 * h + 1 : 3 * h + 2, :]
            ds = (weights * (probs_t[h, slot] - stat[3 * h + 2 : 3 * h + 3, :]) * scaling).astype(BF)
            far_dk[h] = far_dk[h] + dot_nt(qd_far[slot, head(h), :], ds)
            far_dv[h] = far_dv[h] + dot_nt(qd_far[slot, head(h, 1), :], weights.astype(BF))

    key_terms(mid, stat_send[...])
    near_first = far_first[::-1]
    for step in near_first:
        stat_copy(step).wait_recv()
        key_terms((mid - step) % n_seq, stat_recv[step - 1])
    for h in range(2):
        for part, far_part in ((0, far_dk), (1, far_dv)):
            for half in range(2):
                term = near_terms[h][part][:, far_at(half)]
                if half == h:
                    term = term + far_part[h]
                d_parts[2 + part, head(h), far_at(half)] = term.astype(BF)

    y_start(1)
    d_rows = jnp.zeros((BLOCK, n_mp * LANES), F32)
    for part in range(3):
        d_part = dot_nt(eye, d_parts[1 + part]).astype(BF)
        d_rows = d_rows + dot_nn(d_part, weight_pad[part * GROUP : (part + 1) * GROUP, :])
    d_rows = d_rows.astype(BF).astype(F32)
    gain_terms = jnp.sum(d_rows * form_pad[...], axis=0, keepdims=True)
    for m in range(n_mp):
        gm_send[m] = gain_terms[:, m * LANES : (m + 1) * LANES]

    def gm_copy(step):
        to = lax.rem(m_me + step, n_mp)
        return remote(
            gm_send.at[to], gm_recv.at[step - 1], gm_ss.at[step - 1], gm_rs.at[step - 1], {"mp": to}
        )

    def gy_copy(step):
        return remote(
            gy_send, gy_recv.at[step - 1], gy_ss.at[step - 1], gy_rs.at[step - 1],
            peer("dp", d_me, n_dp, step),
        )

    for step in range(1, n_mp):
        go(gm_copy(step))
    z_start(0)
    z_go(0)
    scaled_rows = d_rows * gain_pad[...]
    first = row_sum(scaled_rows)
    second = row_sum(scaled_rows * form_pad[...])
    lane = iota((BLOCK, LANES), 1)
    extra = jnp.zeros((BLOCK, LANES), F32)
    for at, value in ((GROUP, first), (GROUP + 2, second)):
        coarse = value.astype(BF).astype(F32)
        extra = jnp.where(lane == at, coarse, extra)
        extra = jnp.where(lane == at + 1, value - coarse, extra)
    for m in range(n_mp):
        mp_send[m] = (d_rows[:, m * LANES : (m + 1) * LANES] + extra).astype(BF)

    def mp_copy(step):
        to = lax.rem(m_me + step, n_mp)
        return remote(
            mp_send.at[to], mp_recv.at[step - 1], mp_ss.at[step - 1], mp_rs.at[step - 1], {"mp": to}
        )

    for step in range(1, n_mp):
        go(mp_copy(step))
    gain_total = gm_send[m_me]
    for step in range(1, n_mp):
        gm_copy(step).wait_recv()
        gain_total = gain_total + gm_recv[step - 1]
    gy_send[...] = gain_total
    for step in range(1, n_dp):
        go(gy_copy(step))
    z_start(1)
    for step in range(1, n_dp):
        gy_copy(step).wait_recv()
        gain_total = gain_total + gy_recv[step - 1]
    coarse = gain_total.astype(BF).astype(F32)
    spare = iota((n_seq * rows_pad, LANES), 0) % rows_pad == rows
    for at, value in enumerate((coarse, gain_total - coarse)):
        lanes_at = slice(at * LANES, (at + 1) * LANES)
        z_send[1, :, lanes_at] = jnp.where(
            spare, value, z_send[1, :, lanes_at].astype(F32)
        ).astype(BF)
    z_go(1)

    d_normed = mp_send[m_me].astype(F32)
    for step in range(1, n_mp):
        mp_copy(step).wait_recv()
        d_normed = d_normed + mp_recv[step - 1].astype(F32)
    own = pl.ds(pl.multiple_of(m_me * LANES, LANES), LANES)
    form = form_pad[:, own]
    mean_scaled = (d_normed[:, GROUP : GROUP + 1] + d_normed[:, GROUP + 1 : GROUP + 2]) * (1.0 / width)
    mean_mixed = (d_normed[:, GROUP + 2 : GROUP + 3] + d_normed[:, GROUP + 3 : GROUP + 4]) * (1.0 / width)
    scaled = d_normed * gain_pad[:, own]
    d_tok = own_parts[0] + (scaled - mean_scaled - form * mean_mixed) * inverse_std
    turned = dot_nt(eye[:LANES, :LANES], d_tok.astype(BF)).astype(BF)
    tok_out[...] = dot_nn(turned, order).astype(BF)[:GROUP, :]
    for copy in started[: 1 - n_seq]:
        copy.wait_send()
    early = z_end(0)
    qkv_out[:, 0, :] = early[:rows, LANES : LANES + GROUP]
    out_out[...] = early[:rows, :GROUP]
    late = z_end(1)
    qkv_out[:, 1, :] = late[:rows, :GROUP]
    qkv_out[:, 2, :] = late[:rows, LANES : LANES + GROUP]
    gain_out[...] = late[rows : rows + 1, :GROUP] + late[rows : rows + 1, LANES : LANES + GROUP]
    for copy in started[1 - n_seq :]:
        copy.wait_send()


def per_device(n_seq, n_mp, n_dp, tokens, gain, qkv_weight, out_weight, counts, grad_out):
    width = n_mp * GROUP
    chunk = width // n_dp
    rows = chunk // n_seq
    rows_pad = -(-rows // 16) * 16
    mid = n_seq // 2
    weight = qkv_weight.transpose(1, 2, 0).reshape(3 * GROUP, width)
    vmem = pl.BlockSpec(memory_space=pltpu.VMEM)
    dma = pltpu.SemaphoreType.DMA
    far_block = pltpu.VMEM((n_seq, 2 * GROUP, HALF), BF)
    far_square = pltpu.VMEM((2, n_seq, HALF, HALF), F32)
    scratch = [
        pltpu.VMEM((BLOCK, width), BF),
        pltpu.VMEM((BLOCK, width), BF),
        pltpu.VMEM((width,), F32),
        pltpu.VMEM((3 * GROUP, width), BF),
        pltpu.VMEM((GROUP, width), BF),
        far_block, far_block, far_square, far_square, far_square, far_square,
        pltpu.VMEM((2, HALF, HALF), F32),
        pltpu.VMEM((2 * GROUP, BLOCK), BF),
        pltpu.VMEM((2 * GROUP, BLOCK), BF),
        pltpu.VMEM((2, BLOCK, HDIM), BF),
        pltpu.VMEM((2, BLOCK, HDIM), BF),
        pltpu.VMEM((2, HALF, HDIM), BF),
        pltpu.VMEM((2, HALF, HDIM), BF),
        pltpu.VMEM((2, BLOCK, BLOCK), F32),
        pltpu.VMEM((2, BLOCK, BLOCK), F32),
        pltpu.VMEM((BLOCK, width), BF),
        pltpu.VMEM((BLOCK, width), BF),
        pltpu.VMEM((width, BLOCK), BF),
        pltpu.VMEM((width, BLOCK), BF),
        pltpu.VMEM((1, n_mp * LANES), F32),
        pltpu.VMEM((BLOCK, n_mp * LANES), F32),
        pltpu.VMEM((3 * GROUP, n_mp * LANES), BF),
        pltpu.VMEM((4, GROUP, BLOCK), BF),
        pltpu.VMEM((1, BLOCK, LANES), F32),
        pltpu.VMEM((8, LANES), F32),
        pltpu.VMEM((n_seq - 1, 8, LANES), F32),
        pltpu.VMEM((2, n_dp - 1, chunk, BLOCK), BF),
        pltpu.VMEM((2, n_dp - 1, 2, GROUP, BLOCK), BF),
        pltpu.VMEM((2, n_seq * rows_pad, 2 * LANES), BF),
        pltpu.VMEM((2, n_seq - 1, rows_pad, 2 * LANES), BF),
        pltpu.VMEM((n_mp, BLOCK, LANES), BF),
        pltpu.VMEM((n_mp - 1, BLOCK, LANES), BF),
        pltpu.VMEM((n_mp, 1, LANES), F32),
        pltpu.VMEM((n_mp - 1, 1, LANES), F32),
        pltpu.VMEM((1, LANES), F32),
        pltpu.VMEM((n_dp - 1, 1, LANES), F32),
        dma((5,)),
    ]
    for shape in (
        (n_seq // 4, 2, 2, 2), (n_seq // 4, 2, 2, 2), (n_seq - 1,), (2, n_dp - 1), (2, n_dp - 1), (2, n_seq - 1), (n_mp - 1,),
        (n_mp - 1,), (n_dp - 1,),
    ):
        scratch += [dma(shape), dma(shape)]
    shapes = (
        jax.ShapeDtypeStruct((GROUP, BLOCK), BF),
        jax.ShapeDtypeStruct((rows, 3, GROUP), F32),
        jax.ShapeDtypeStruct((rows, GROUP), F32),
        jax.ShapeDtypeStruct((1, GROUP), F32),
    )
    anywhere = pl.BlockSpec(memory_space=pl.ANY)
    results = pl.pallas_call(
        functools.partial(layer_kernel, n_seq, n_mp, n_dp),
        out_shape=shapes,
        in_specs=[pl.BlockSpec(memory_space=pltpu.SMEM)] + [anywhere] * 5,
        out_specs=(vmem,) * 4,
        scratch_shapes=scratch,
        compiler_params=pltpu.CompilerParams(
            collective_id=0, has_side_effects=True, vmem_limit_bytes=VMEM_BYTES
        ),
    )(counts, tokens[0], grad_out[0], gain, weight, out_weight)
    tok_turned, d_qkv, out_turned, d_gain = pl.pallas_call(
        hand_on,
        out_shape=shapes,
        in_specs=[vmem] * 4,
        out_specs=(vmem,) * 4,
        compiler_params=pltpu.CompilerParams(vmem_limit_bytes=VMEM_BYTES),
    )(*results)
    return (tok_turned.T[None], d_qkv, out_turned.T, d_gain[0])


def hand_on(*refs):
    for at in range(4):
        refs[4 + at][...] = refs[at][...]


def solution(mesh):
    sizes = (mesh.shape["seq"], mesh.shape["mp"], mesh.shape["dp"])
    placed = (
        P("dp", "seq", None),
        P(),
        P(None, None, "mp"),
        P("mp", None),
        P("dp"),
        P("dp", "seq", None),
    )
    return jax.shard_map(
        functools.partial(per_device, *sizes),
        mesh=mesh,
        in_specs=placed,
        out_specs=(
            P("dp", "seq", "mp"),
            P(("seq", "dp"), None, "mp"),
            P("mp", ("seq", "dp")),
            P("mp"),
        ),
        check_vma=False,
    )
```

```python
import functools
import math

import jax
import jax.numpy as jnp
from jax import lax
from jax.experimental import pallas as pl
from jax.experimental.pallas import tpu as pltpu
from jax.sharding import PartitionSpec as P

HDIM = 48
BLOCK = 256
HALF = BLOCK // 2
GROUP = 2 * HDIM
LANES = 128
VMEM_BYTES = 60 * 1024 * 1024
MESH = pl.DeviceIdType.MESH
BF = jnp.bfloat16
F32 = jnp.float32
far_below = -1e30


def dot_nn(left, right):
    return lax.dot_general(left, right, (((1,), (0,)), ((), ())), preferred_element_type=F32)


def dot_nt(left, right):
    return lax.dot_general(left, right, (((1,), (1,)), ((), ())), preferred_element_type=F32)


def iota(shape, axis):
    return lax.broadcasted_iota(jnp.int32, shape, axis)


def one_hot(condition):
    return jnp.where(condition, 1.0, 0.0).astype(BF)


def row_sum(value):
    return jnp.sum(value, axis=1, keepdims=True)


def floor_div(value, by):
    return jnp.floor((value + 0.5) * (1.0 / by))


def layer_kernel(
    n_seq, n_mp, n_dp,
    counts, tokens_hbm, grad_hbm, gain_hbm, weight_hbm, out_weight_hbm,
    tok_hbm, qkv_hbm, out_hbm, gain_hbm_out,
    tok_out, qkv_out, out_out, gain_out, out_sem,
    tokens, grad_out, gain, weight, out_weight,
    kv_far, qd_far, scores, probs, scores_t, probs_t, top, kv_here, qd_here, q_rows, da_rows, k_rows, v_rows,
    near_scores, near_probs, normed_s, go_s, normed_p, go_p, gain_pad, form_pad, weight_pad,
    d_parts, own_parts, stat_send, stat_recv,
    side_recv, y_recv, z_send, z_recv, mp_send, mp_recv,
    gm_send, gm_recv, gy_send, gy_recv,
    in_sem, kv_ss, kv_rs, qd_ss, qd_rs, st_ss, st_rs, sd_ss, sd_rs, y_ss, y_rs, z_ss, z_rs, mp_ss, mp_rs,
    gm_ss, gm_rs, gy_ss, gy_rs,
):
    width = n_mp * GROUP
    chunk = width // n_dp
    rows = chunk // n_seq
    rows_pad = -(-rows // 16) * 16
    mid = n_seq // 2
    scaling = 1.0 / math.sqrt(HDIM)
    s_me = lax.axis_index("seq")
    m_me = lax.axis_index("mp")
    d_me = lax.axis_index("dp")
    count = counts[0]

    loads = [
        pltpu.make_async_copy(source, target, in_sem.at[at])
        for at, (source, target) in enumerate((
            (tokens_hbm, tokens), (gain_hbm, gain), (weight_hbm, weight),
            (grad_hbm, grad_out), (out_weight_hbm, out_weight),
        ))
    ]
    for load in loads:
        load.start()

    def peer(axis, me, size, step):
        return {axis: lax.rem(me + (step + size), size)}

    barrier = pltpu.get_barrier_semaphore()
    greeted = [("seq", s_me, n_seq, step) for step in sorted({2, n_seq - 2, 1, n_seq - 1})]
    greeted += [("dp", d_me, n_dp, step) for step in range(1, n_dp)]
    greeted += [("mp", m_me, n_mp, step) for step in range(1, n_mp)]
    for other in greeted:
        pl.semaphore_signal(barrier, inc=1, device_id=peer(*other), device_id_type=MESH)

    started = []

    def remote(src, dst, send, recv, device):
        return pltpu.make_async_remote_copy(
            src_ref=src, dst_ref=dst, send_sem=send, recv_sem=recv,
            device_id=device, device_id_type=MESH,
        )

    def go(copy):
        copy.start()
        started.append(copy)

    def position(shape, axis):
        at = iota(shape, axis)
        return 2 * (at % HALF) + at // HALF

    def head(h, part=0):
        return slice(part * GROUP + h * HDIM, part * GROUP + (h + 1) * HDIM)

    def far_at(h):
        return slice(h * HALF, (h + 1) * HALF)

    order = one_hot(position((BLOCK, BLOCK), 0) == iota((BLOCK, BLOCK), 1))
    eye = one_hot(iota((BLOCK, BLOCK), 0) == iota((BLOCK, BLOCK), 1))

    loads[0].wait()
    x = dot_nn(order, tokens[...])
    mean = row_sum(x) * (1.0 / width)
    centered = x - mean
    inverse_std = lax.rsqrt(row_sum(centered * centered) * (1.0 / width) + 1e-05)
    normal_form = centered * inverse_std
    loads[1].wait()
    normed = (normal_form * gain[...].reshape(1, width)).astype(BF)
    normed_s[...] = normed
    loads[2].wait()
    kv_here[...] = dot_nt(weight[GROUP:, :], normed).astype(BF)
    for part in range(2):
        for h in range(2):
            kv_far[mid, head(h, part), :] = kv_here[head(h, part), far_at(h)]

    pl.semaphore_wait(barrier, len(greeted))

    def seq_peer(step):
        return peer("seq", s_me, n_seq, step)

    def gather_copy(which, stage, way, far, piece):
        blocks, send, recv = gathers[which]
        sign = 1 - 2 * way
        source, target = mid - sign * 2 * stage, mid - sign * (2 * stage + far)
        at = pl.ds(piece * GROUP, GROUP)
        return remote(
            blocks.at[source % n_seq, at], blocks.at[target % n_seq, at],
            send.at[stage, way, far - 1, piece], recv.at[stage, way, far - 1, piece],
            seq_peer(sign * far),
        )

    gathers = ((kv_far, kv_ss, kv_rs), (qd_far, qd_ss, qd_rs))

    def moves(stage):
        return [
            (stage, way, far, piece)
            for far in (2, 1) for piece in range(2) for way in range(2)
            if 2 * stage + far < mid or (2 * stage + far == mid and way == piece)
        ]

    def gather_stage(which, stage):
        for move in moves(stage):
            if move[2] == 2:
                gather_copy(which, *move).wait_recv()
                for later in (moves(stage + 1) if 2 * stage + 2 < mid else []):
                    if (later[1], later[3]) == (move[1], move[3]):
                        go(gather_copy(which, *later))
        for move in moves(stage):
            if move[2] == 1:
                gather_copy(which, *move).wait_recv()

    for move in moves(0):
        go(gather_copy(0, *move))
    qd_here[:GROUP, :] = dot_nt(weight[:GROUP, :], normed).astype(BF)
    for load in loads[3:]:
        load.wait()
    go_s[...] = dot_nn(order, grad_out[...]).astype(BF)
    qd_here[GROUP:, :] = dot_nt(out_weight[...], go_s[...]).astype(BF)
    for part in range(2):
        for h in range(2):
            qd_far[mid, head(h, part), :] = qd_here[head(h, part), far_at(h)]
    for move in moves(0):
        go(gather_copy(1, *move))

    live_key = s_me * BLOCK + position((1, BLOCK), 1) < count
    live_query = s_me * BLOCK + position((BLOCK, 1), 0) < count
    for h in range(2):
        q_rows[h] = dot_nt(eye, qd_here[head(h), :]).astype(BF)
        da_rows[h] = dot_nt(eye, qd_here[head(h, 1), :]).astype(BF)
        k_rows[h] = dot_nt(eye[:HALF, :HALF], kv_far[mid, head(h), :]).astype(BF)
        v_rows[h] = dot_nt(eye[:HALF, :HALF], kv_far[mid, head(h, 1), :]).astype(BF)
        near_scores[h] = jnp.where(
            live_key, dot_nn(q_rows[h], kv_here[head(h), :]) * scaling, far_below
        )
        near_probs[h] = dot_nn(da_rows[h], kv_here[head(h, 1), :])
        top[h] = jnp.maximum(
            near_scores[h, far_at(h), :HALF], near_scores[h, far_at(h), HALF:]
        )

    def far_scores(slot):
        owner = lax.rem(s_me + (slot - mid + n_seq), n_seq)
        for h in range(2):
            live = owner * BLOCK + 2 * iota((1, HALF), 1) + h < count
            score = dot_nn(q_rows[h, far_at(h), :], kv_far[slot, head(h), :]) * scaling
            score = jnp.where(live, score, far_below)
            scores[h, slot] = score
            top[h] = jnp.maximum(top[h], score)
            probs[h, slot] = dot_nn(da_rows[h, far_at(h), :], kv_far[slot, head(h, 1), :])

    def turned_scores(slot):
        for h in range(2):
            live = s_me * BLOCK + 2 * iota((HALF, 1), 0) + h < count
            score = dot_nn(k_rows[h], qd_far[slot, head(h), :]) * scaling
            scores_t[h, slot] = jnp.where(live, score, far_below)
            probs_t[h, slot] = dot_nn(v_rows[h], qd_far[slot, head(h, 1), :])

    place = iota((width, 1), 0).astype(F32)
    piece_at = floor_div(place, rows)
    dp_at = floor_div(piece_at, n_seq)
    feature = n_dp * rows * (piece_at - n_seq * dp_at) + rows * dp_at + (place - rows * piece_at)
    spread = one_hot(feature == iota((width, width), 1).astype(F32))

    def fill_pads():
        for m in range(n_mp):
            to, of = pl.ds(m * LANES, GROUP), slice(m * GROUP, (m + 1) * GROUP)
            rest = pl.ds(m * LANES + GROUP, LANES - GROUP)
            form_pad[:, to] = normal_form[:, of]
            form_pad[:, rest] = jnp.zeros((BLOCK, LANES - GROUP), F32)
            gain_pad[:, to] = gain[...].reshape(1, width)[:, of]
            gain_pad[:, rest] = jnp.zeros((1, LANES - GROUP), F32)

    def chunk_of(device):
        return pl.ds(pl.multiple_of(device * chunk, 16), chunk)

    def side_copy(side, step):
        to = lax.rem(d_me + step, n_dp)
        return remote(
            (go_p, normed_p)[side].at[chunk_of(to)], side_recv.at[side, step - 1],
            sd_ss.at[side, step - 1], sd_rs.at[side, step - 1], {"dp": to},
        )

    def fill_normed():
        normed_p[...] = dot_nt(spread, normed_s[...]).astype(BF)
        for step in range(1, n_dp):
            go(side_copy(1, step))

    def fill_go():
        go_p[...] = dot_nt(spread, go_s[...]).astype(BF)
        for step in range(1, n_dp):
            go(side_copy(0, step))

    def fill_weight():
        for m in range(n_mp):
            weight_pad[:, m * LANES : m * LANES + GROUP] = weight[:, m * GROUP : (m + 1) * GROUP]
            weight_pad[:, m * LANES + GROUP : (m + 1) * LANES] = jnp.zeros(
                (3 * GROUP, LANES - GROUP), BF
            )

    def fill_own():
        mine = one_hot(
            (iota((width, LANES), 0) == m_me * GROUP + iota((width, LANES), 1))
            & (iota((width, LANES), 1) < GROUP)
        )
        own_parts[0] = dot_nn(go_s[...], mine)
        z_send[...] = jnp.zeros(z_send.shape, BF)

    fillers = [fill_pads, fill_normed, fill_go, fill_weight, fill_own]

    def stage_slots(stage):
        aways = (2 * stage + 1, 2 * stage + 2)
        return [mid - away for away in aways] + [mid + away for away in aways if away < mid]

    far_scores(mid)
    turned_scores(mid)
    stages = n_seq // 4
    lag = min(1, stages - 1)
    done = [mid]
    for stage in range(stages - 1):
        gather_stage(0, stage)
        if stage >= lag:
            gather_stage(1, stage - lag)
        for slot in stage_slots(stage):
            far_scores(slot)
            done.append(slot)
        if stage >= lag:
            for slot in stage_slots(stage - lag):
                turned_scores(slot)
        for _ in range(2):
            if fillers:
                fillers.pop(0)()
    for filler in fillers:
        filler()

    def grow(h, slots, peak):
        total = jnp.zeros((HALF, HALF), F32)
        delta = jnp.zeros((HALF, HALF), F32)
        for slot in slots:
            grown = jnp.exp(scores[h, slot] - peak)
            scores[h, slot] = grown
            total = total + grown
            delta = delta + grown * probs[h, slot]
        return row_sum(total), row_sum(delta)

    first_peaks, first_sums = [], []
    for h in range(2):
        peaks, sums = [], []
        for half in range(2):
            at = far_at(half)
            near = near_scores[h, at, :]
            peak = jnp.max(top[h] if half == h else near, axis=1, keepdims=True)
            grown = jnp.exp(near - peak)
            near_scores[h, at, :] = grown
            total, delta = row_sum(grown), row_sum(grown * near_probs[h, at, :])
            if half == h:
                far_total, far_delta = grow(h, done, peak)
                total, delta = total + far_total, delta + far_delta
            peaks.append(peak)
            sums.append((total, delta))
        first_peaks.append(peaks)
        first_sums.append(sums)

    gather_stage(0, stages - 1)
    last = stage_slots(stages - 1)
    for slot in last:
        far_scores(slot)
    inverse_total, inverse_first, deltas = [], [], []
    lane = iota((HALF, LANES), 1)
    stats = jnp.zeros((HALF, LANES), F32)
    for h in range(2):
        far_top = jnp.max(top[h], axis=1, keepdims=True)
        shrink = jnp.exp(first_peaks[h][h] - far_top)
        last_total, last_delta = grow(h, last, far_top)
        total, delta = first_sums[h][h]
        inverse = jnp.where(
            live_query[far_at(h), :], 1.0 / (total * shrink + last_total), 0.0
        )
        far_delta = (delta * shrink + last_delta) * inverse
        total, delta = first_sums[h][1 - h]
        other = jnp.where(live_query[far_at(1 - h), :], 1.0 / total, 0.0)
        pairs = [(shrink * inverse, far_delta), (other, delta * other)]
        inverse_total.append(inverse)
        inverse_first.append([pairs[half != h][0] for half in range(2)])
        deltas.append([pairs[half != h][1] for half in range(2)])
        for at, value in enumerate((far_top, inverse, far_delta)):
            stats = jnp.where(lane == 3 * h + at, value, stats)
    stat_send[...] = jnp.transpose(stats)[:8, :]

    def stat_copy(step):
        return remote(
            stat_send, stat_recv.at[step - 1], st_ss.at[step - 1], st_rs.at[step - 1], seq_peer(step)
        )

    far_first = sorted(range(1, n_seq), key=lambda step: -min(step, n_seq - step))
    for step in far_first:
        go(stat_copy(step))

    attended = [jnp.zeros((HDIM, HALF), F32) for _ in range(2)]
    d_query = [jnp.zeros((HDIM, HALF), F32) for _ in range(2)]

    def far_terms(slot):
        for h in range(2):
            weights = scores[h, slot] * (inverse_total[h] if slot in last else inverse_first[h][h])
            ds = (weights * (probs[h, slot] - deltas[h][h]) * scaling).astype(BF)
            attended[h] = attended[h] + dot_nt(kv_far[slot, head(h, 1), :], weights.astype(BF))
            d_query[h] = d_query[h] + dot_nt(kv_far[slot, head(h), :], ds)

    near_terms = []

    def near_part():
        for h in range(2):
            weights = near_scores[h] * jnp.concatenate(inverse_first[h], axis=0)
            bar = weights.astype(BF)
            delta = jnp.concatenate(deltas[h], axis=0)
            ds = (weights * (near_probs[h] - delta) * scaling).astype(BF)
            near_terms.append((dot_nn(qd_here[head(h), :], ds), dot_nn(qd_here[head(h, 1), :], bar)))
            near_att = dot_nt(kv_here[head(h, 1), :], bar)
            near_dq = dot_nt(kv_here[head(h), :], ds)
            for half in range(2):
                at = far_at(half)
                att, dq = near_att[:, at], near_dq[:, at]
                if half == h:
                    att, dq = att + attended[h], dq + d_query[h]
                d_parts[0, head(h), at] = att.astype(BF)
                d_parts[1, head(h), at] = dq.astype(BF)

    def y_copy(phase, step):
        return remote(
            d_parts.at[pl.ds(2 * phase, 2)], y_recv.at[phase, step - 1],
            y_ss.at[phase, step - 1], y_rs.at[phase, step - 1], peer("dp", d_me, n_dp, step),
        )

    def z_copy(phase, step):
        to = lax.rem(s_me + step, n_seq)
        at = pl.ds(pl.multiple_of(to * rows_pad, 16), rows_pad)
        return remote(
            z_send.at[phase, at], z_recv.at[phase, step - 1],
            z_ss.at[phase, step - 1], z_rs.at[phase, step - 1], {"seq": to},
        )

    def y_start(phase):
        for step in range(1, n_dp):
            go(y_copy(phase, step))

    widen = one_hot(
        (iota((n_seq * rows_pad, chunk), 0) // rows_pad * rows
         + iota((n_seq * rows_pad, chunk), 0) % rows_pad == iota((n_seq * rows_pad, chunk), 1))
        & (iota((n_seq * rows_pad, chunk), 0) % rows_pad < rows)
    )

    def z_start(phase):
        mine = chunk_of(d_me)
        sides = ((go_p, 0), (normed_p, 1)) if phase == 0 else ((normed_p, 1), (normed_p, 1))
        if phase == 0:
            for side in range(2):
                for step in range(1, n_dp):
                    side_copy(side, step).wait_recv()
        sums = [dot_nt(side[mine, :], d_parts[2 * phase + at]) for at, (side, _) in enumerate(sides)]
        for step in range(1, n_dp):
            y_copy(phase, step).wait_recv()
            for at, (_, side) in enumerate(sides):
                sums[at] = sums[at] + dot_nt(side_recv[side, step - 1], y_recv[phase, step - 1, at])
        for at in range(2):
            z_send[phase, :, at * LANES : at * LANES + GROUP] = dot_nn(
                widen, sums[at].astype(BF)
            ).astype(BF)

    def z_go(phase):
        for step in far_first:
            go(z_copy(phase, step))

    def z_end(phase):
        mine = pl.ds(pl.multiple_of(s_me * rows_pad, 16), rows_pad)
        total = z_send[phase, mine, :].astype(F32)
        for step in far_first[::-1]:
            z_copy(phase, step).wait_recv()
            total = total + z_recv[phase, step - 1].astype(F32)
        return total

    for stage in range(stages - 1 - lag, stages - 1):
        gather_stage(1, stage)
    for slot in range(n_seq):
        far_terms(slot)
    near_part()
    y_start(0)
    for stage in range(stages - 1 - lag, stages - 1):
        for slot in stage_slots(stage):
            turned_scores(slot)

    far_dk = [jnp.zeros((HDIM, HALF), F32) for _ in range(2)]
    far_dv = [jnp.zeros((HDIM, HALF), F32) for _ in range(2)]

    def key_terms(slot, stat):
        for h in range(2):
            weights = jnp.exp(scores_t[h, slot] - stat[3 * h : 3 * h + 1, :]) * stat[3 * h + 1 : 3 * h + 2, :]
            ds = (weights * (probs_t[h, slot] - stat[3 * h + 2 : 3 * h + 3, :]) * scaling).astype(BF)
            far_dk[h] = far_dk[h] + dot_nt(qd_far[slot, head(h), :], ds)
            far_dv[h] = far_dv[h] + dot_nt(qd_far[slot, head(h, 1), :], weights.astype(BF))

    key_terms(mid, stat_send[...])
    near_first = far_first[::-1]
    for at, step in enumerate(near_first):
        if at == n_seq - 1 - len(last):
            gather_stage(1, stages - 1)
            for slot in last:
                turned_scores(slot)
        stat_copy(step).wait_recv()
        key_terms((mid - step) % n_seq, stat_recv[step - 1])
    for h in range(2):
        for part, far_part in ((0, far_dk), (1, far_dv)):
            for half in range(2):
                term = near_terms[h][part][:, far_at(half)]
                if half == h:
                    term = term + far_part[h]
                d_parts[2 + part, head(h), far_at(half)] = term.astype(BF)

    y_start(1)
    d_rows = jnp.zeros((BLOCK, n_mp * LANES), F32)
    for part in range(3):
        d_part = dot_nt(eye, d_parts[1 + part]).astype(BF)
        d_rows = d_rows + dot_nn(d_part, weight_pad[part * GROUP : (part + 1) * GROUP, :])
    d_rows = d_rows.astype(BF).astype(F32)
    gain_terms = jnp.sum(d_rows * form_pad[...], axis=0, keepdims=True)
    for m in range(n_mp):
        gm_send[m] = gain_terms[:, m * LANES : (m + 1) * LANES]

    def gm_copy(step):
        to = lax.rem(m_me + step, n_mp)
        return remote(
            gm_send.at[to], gm_recv.at[step - 1], gm_ss.at[step - 1], gm_rs.at[step - 1], {"mp": to}
        )

    def gy_copy(step):
        return remote(
            gy_send, gy_recv.at[step - 1], gy_ss.at[step - 1], gy_rs.at[step - 1],
            peer("dp", d_me, n_dp, step),
        )

    for step in range(1, n_mp):
        go(gm_copy(step))
    z_start(0)
    z_go(0)
    scaled_rows = d_rows * gain_pad[...]
    first = row_sum(scaled_rows)
    second = row_sum(scaled_rows * form_pad[...])
    lane = iota((BLOCK, LANES), 1)
    extra = jnp.zeros((BLOCK, LANES), F32)
    for at, value in ((GROUP, first), (GROUP + 2, second)):
        coarse = value.astype(BF).astype(F32)
        extra = jnp.where(lane == at, coarse, extra)
        extra = jnp.where(lane == at + 1, value - coarse, extra)
    for m in range(n_mp):
        mp_send[m] = (d_rows[:, m * LANES : (m + 1) * LANES] + extra).astype(BF)

    def mp_copy(step):
        to = lax.rem(m_me + step, n_mp)
        return remote(
            mp_send.at[to], mp_recv.at[step - 1], mp_ss.at[step - 1], mp_rs.at[step - 1], {"mp": to}
        )

    for step in range(1, n_mp):
        go(mp_copy(step))
    gain_total = gm_send[m_me]
    for step in range(1, n_mp):
        gm_copy(step).wait_recv()
        gain_total = gain_total + gm_recv[step - 1]
    gy_send[...] = gain_total
    for step in range(1, n_dp):
        go(gy_copy(step))
    z_start(1)
    for step in range(1, n_dp):
        gy_copy(step).wait_recv()
        gain_total = gain_total + gy_recv[step - 1]
    coarse = gain_total.astype(BF).astype(F32)
    spare = iota((n_seq * rows_pad, LANES), 0) % rows_pad == rows
    for at, value in enumerate((coarse, gain_total - coarse)):
        lanes_at = slice(at * LANES, (at + 1) * LANES)
        z_send[1, :, lanes_at] = jnp.where(
            spare, value, z_send[1, :, lanes_at].astype(F32)
        ).astype(BF)
    z_go(1)

    d_normed = mp_send[m_me].astype(F32)
    for step in range(1, n_mp):
        mp_copy(step).wait_recv()
        d_normed = d_normed + mp_recv[step - 1].astype(F32)
    own = pl.ds(pl.multiple_of(m_me * LANES, LANES), LANES)
    form = form_pad[:, own]
    mean_scaled = (d_normed[:, GROUP : GROUP + 1] + d_normed[:, GROUP + 1 : GROUP + 2]) * (1.0 / width)
    mean_mixed = (d_normed[:, GROUP + 2 : GROUP + 3] + d_normed[:, GROUP + 3 : GROUP + 4]) * (1.0 / width)
    scaled = d_normed * gain_pad[:, own]
    d_tok = own_parts[0] + (scaled - mean_scaled - form * mean_mixed) * inverse_std
    turned = dot_nt(eye[:LANES, :LANES], d_tok.astype(BF)).astype(BF)
    tok_out[...] = dot_nn(turned, order).astype(BF)[:GROUP, :]
    stores = [
        pltpu.make_async_copy(source, target, out_sem.at[at])
        for at, (source, target) in enumerate((
            (tok_out, tok_hbm), (qkv_out, qkv_hbm), (out_out, out_hbm), (gain_out, gain_hbm_out),
        ))
    ]
    stores[0].start()
    for copy in started[: 1 - n_seq]:
        copy.wait_send()
    early = z_end(0)
    qkv_out[:, 0, :] = early[:rows, LANES : LANES + GROUP]
    out_out[...] = early[:rows, :GROUP]
    late = z_end(1)
    qkv_out[:, 1, :] = late[:rows, :GROUP]
    qkv_out[:, 2, :] = late[:rows, LANES : LANES + GROUP]
    gain_out[...] = late[rows : rows + 1, :GROUP] + late[rows : rows + 1, LANES : LANES + GROUP]
    for store in stores[1:]:
        store.start()
    for copy in started[1 - n_seq :]:
        copy.wait_send()
    for store in stores:
        store.wait()


def per_device(n_seq, n_mp, n_dp, tokens, gain, qkv_weight, out_weight, counts, grad_out):
    width = n_mp * GROUP
    chunk = width // n_dp
    rows = chunk // n_seq
    rows_pad = -(-rows // 16) * 16
    mid = n_seq // 2
    weight = qkv_weight.transpose(1, 2, 0).reshape(3 * GROUP, width)
    vmem = pl.BlockSpec(memory_space=pltpu.VMEM)
    dma = pltpu.SemaphoreType.DMA
    far_block = pltpu.VMEM((n_seq, 2 * GROUP, HALF), BF)
    far_square = pltpu.VMEM((2, n_seq, HALF, HALF), F32)
    scratch = [
        pltpu.VMEM((GROUP, BLOCK), BF),
        pltpu.VMEM((rows, 3, GROUP), F32),
        pltpu.VMEM((rows, GROUP), F32),
        pltpu.VMEM((1, GROUP), F32),
        dma((4,)),
        pltpu.VMEM((BLOCK, width), BF),
        pltpu.VMEM((BLOCK, width), BF),
        pltpu.VMEM((width,), F32),
        pltpu.VMEM((3 * GROUP, width), BF),
        pltpu.VMEM((GROUP, width), BF),
        far_block, far_block, far_square, far_square, far_square, far_square,
        pltpu.VMEM((2, HALF, HALF), F32),
        pltpu.VMEM((2 * GROUP, BLOCK), BF),
        pltpu.VMEM((2 * GROUP, BLOCK), BF),
        pltpu.VMEM((2, BLOCK, HDIM), BF),
        pltpu.VMEM((2, BLOCK, HDIM), BF),
        pltpu.VMEM((2, HALF, HDIM), BF),
        pltpu.VMEM((2, HALF, HDIM), BF),
        pltpu.VMEM((2, BLOCK, BLOCK), F32),
        pltpu.VMEM((2, BLOCK, BLOCK), F32),
        pltpu.VMEM((BLOCK, width), BF),
        pltpu.VMEM((BLOCK, width), BF),
        pltpu.VMEM((width, BLOCK), BF),
        pltpu.VMEM((width, BLOCK), BF),
        pltpu.VMEM((1, n_mp * LANES), F32),
        pltpu.VMEM((BLOCK, n_mp * LANES), F32),
        pltpu.VMEM((3 * GROUP, n_mp * LANES), BF),
        pltpu.VMEM((4, GROUP, BLOCK), BF),
        pltpu.VMEM((1, BLOCK, LANES), F32),
        pltpu.VMEM((8, LANES), F32),
        pltpu.VMEM((n_seq - 1, 8, LANES), F32),
        pltpu.VMEM((2, n_dp - 1, chunk, BLOCK), BF),
        pltpu.VMEM((2, n_dp - 1, 2, GROUP, BLOCK), BF),
        pltpu.VMEM((2, n_seq * rows_pad, 2 * LANES), BF),
        pltpu.VMEM((2, n_seq - 1, rows_pad, 2 * LANES), BF),
        pltpu.VMEM((n_mp, BLOCK, LANES), BF),
        pltpu.VMEM((n_mp - 1, BLOCK, LANES), BF),
        pltpu.VMEM((n_mp, 1, LANES), F32),
        pltpu.VMEM((n_mp - 1, 1, LANES), F32),
        pltpu.VMEM((1, LANES), F32),
        pltpu.VMEM((n_dp - 1, 1, LANES), F32),
        dma((5,)),
    ]
    for shape in (
        (n_seq // 4, 2, 2, 2), (n_seq // 4, 2, 2, 2), (n_seq - 1,), (2, n_dp - 1), (2, n_dp - 1), (2, n_seq - 1), (n_mp - 1,),
        (n_mp - 1,), (n_dp - 1,),
    ):
        scratch += [dma(shape), dma(shape)]
    shapes = (
        jax.ShapeDtypeStruct((GROUP, BLOCK), BF),
        jax.ShapeDtypeStruct((rows, 3, GROUP), F32),
        jax.ShapeDtypeStruct((rows, GROUP), F32),
        jax.ShapeDtypeStruct((1, GROUP), F32),
    )
    anywhere = pl.BlockSpec(memory_space=pl.ANY)
    results = pl.pallas_call(
        functools.partial(layer_kernel, n_seq, n_mp, n_dp),
        out_shape=shapes,
        in_specs=[pl.BlockSpec(memory_space=pltpu.SMEM)] + [anywhere] * 5,
        out_specs=(anywhere,) * 4,
        scratch_shapes=scratch,
        compiler_params=pltpu.CompilerParams(
            collective_id=0, has_side_effects=True, vmem_limit_bytes=VMEM_BYTES
        ),
    )(counts, tokens[0], grad_out[0], gain, weight, out_weight)
    tok_turned, d_qkv, out_turned, d_gain = pl.pallas_call(
        hand_on,
        out_shape=shapes,
        in_specs=[vmem] * 4,
        out_specs=(vmem,) * 4,
        compiler_params=pltpu.CompilerParams(vmem_limit_bytes=VMEM_BYTES),
    )(*results)
    return (tok_turned.T[None], d_qkv, out_turned.T, d_gain[0])


def hand_on(*refs):
    for at in range(4):
        refs[4 + at][...] = refs[at][...]


def solution(mesh):
    sizes = (mesh.shape["seq"], mesh.shape["mp"], mesh.shape["dp"])
    placed = (
        P("dp", "seq", None),
        P(),
        P(None, None, "mp"),
        P("mp", None),
        P("dp"),
        P("dp", "seq", None),
    )
    return jax.shard_map(
        functools.partial(per_device, *sizes),
        mesh=mesh,
        in_specs=placed,
        out_specs=(
            P("dp", "seq", "mp"),
            P(("seq", "dp"), None, "mp"),
            P("mp", ("seq", "dp")),
            P("mp"),
        ),
        check_vma=False,
    )
```
